32 devices in a mesh: dp: 16 (over z, y, x), tensor: 2 (over core).
Axes of the slice: x: 2, y: 2, z: 4, core: 2. Of those that a mesh axis runs over, the one named last changes fastest.
Arguments:
- inputs: bfloat16 [4096, 2560], P(('dp', 'tensor')), may hold values from -6 to 6
- gain_mix: bfloat16 [2560], P('dp'), may hold values from 0.099609375 to 1.8984375
- gain_mlp: bfloat16 [2560], P('dp'), may hold values from 0.099609375 to 1.8984375
- branch_x: bfloat16 [2560, 2560], P('dp', 'tensor'), may hold values from -0.125 to 0.125
- branch_y: bfloat16 [2560, 2560], P('dp', 'tensor'), may hold values from -0.125 to 0.125
- conv_taps: bfloat16 [4, 2560], P(None, ('tensor', 'dp')), may hold values from -3 to 3
- conv_bias: bfloat16 [2560], P(('tensor', 'dp')), may hold values from -3 to 3
- gate_a: bfloat16 [10, 256, 256], P('tensor', 'dp'), may hold values from -0.375 to 0.375
- bias_a: bfloat16 [2560], P(('tensor', 'dp')), may hold values from -4 to 4
- gate_in: bfloat16 [10, 256, 256], P('tensor', 'dp'), may hold values from -0.375 to 0.375
- bias_in: bfloat16 [2560], P(('tensor', 'dp')), may hold values from -4 to 4
- decay_param: bfloat16 [2560], P(('tensor', 'dp')), may hold values from -9 to -4.5
- out_proj: bfloat16 [2560, 2560], P('tensor', 'dp'), may hold values from -0.5 to 0.5
- ffn_gate: bfloat16 [2560, 7680], P('dp', 'tensor'), may hold values from -0.125 to 0.125
- ffn_up: bfloat16 [2560, 7680], P('dp', 'tensor'), may hold values from -0.125 to 0.125
- ffn_down: bfloat16 [7680, 2560], P('tensor', 'dp'), may hold values from -0.125 to 0.125
- cotangent: bfloat16 [4096, 2560], P(('dp', 'tensor')), may hold values from -6 to 6
Outputs:
- result: bfloat16 [4096, 2560], P(('dp', 'tensor'))
- grad_inputs: float32 [4096, 2560], P(('dp', 'tensor'))
- grad_gain_mix: float32 [2560], P(('dp', 'tensor'))
- grad_gain_mlp: float32 [2560], P(('dp', 'tensor'))
- grad_branch_x: float32 [2560, 2560], P('dp', 'tensor')
- grad_branch_y: float32 [2560, 2560], P('dp', 'tensor')
- grad_conv_taps: float32 [4, 2560], P(None, ('tensor', 'dp'))
- grad_conv_bias: float32 [2560], P(('tensor', 'dp'))
- grad_gate_a: float32 [10, 256, 256], P('tensor', 'dp')
- grad_bias_a: float32 [2560], P(('tensor', 'dp'))
- grad_gate_in: float32 [10, 256, 256], P('tensor', 'dp')
- grad_bias_in: float32 [2560], P(('tensor', 'dp'))
- grad_decay_param: float32 [2560], P(('tensor', 'dp'))
- grad_out_proj: float32 [2560, 2560], P('tensor', 'dp')
- grad_ffn_gate: float32 [2560, 7680], P('dp', 'tensor')
- grad_ffn_up: float32 [2560, 7680], P('dp', 'tensor')
- grad_ffn_down: float32 [7680, 2560], P('tensor', 'dp')
The draws below stay inside these ranges and needn't reach their ends.
All inputs are finite; a program needn't handle non-finite values.
Results may differ from the reference program's by a relative error of at most 0.009.
Values may be sent and summed in bfloat16 or wider, within the bound.
No kernel may reach another device: no remote copies, remote signals or barrier semaphores. Data moves between devices by JAX's collectives and lax.ppermute only.
A program may use at most 384 MiB of HBM per device.

```python
import jax
import jax.numpy as jnp
from jax import lax

D = 2560
FF = 7680
HEADS = 10
BLOCK = 256
TAPS = 4
SEQ = 256
LRU = 2560
TOKENS = 4096
N_DP = 16


def spiked(array, rng, source, target, blocks, factor):
    owner, partner = [(jnp.arange(array.shape[position]) // (array.shape[position] // blocks)).reshape([-1 if axis == position else 1 for axis in range(array.ndim)]) for position in (source, target)]
    chosen = jax.random.permutation(rng, blocks)[partner]
    strong = (owner == chosen) | (owner == (partner + blocks // 2) % blocks)
    return jnp.where(strong, factor * array, array)


def steps_of(rng, shape, cuts, smallest, high):
    factor_of, own = 1.0, jax.random.fold_in(rng, 6)
    for dim, parts in cuts:
        heights = jnp.exp(jax.random.uniform(jax.random.fold_in(own, dim), (parts,), jnp.float32, smallest / len(cuts), high / len(cuts)))
        factor_of = factor_of * jnp.repeat(heights, shape[dim] // parts).reshape([-1 if axis == dim else 1 for axis in range(len(shape))])
    return factor_of


def bell_draw(key, shape, spread, reach, shards=(), dtype=jnp.bfloat16):
    drawn = spread * jax.random.normal(key, shape, jnp.float32)
    if shards:
        drawn = drawn * steps_of(key, shape, shards, -0.22, 0.18)
    return jnp.clip(drawn, -reach, reach).astype(dtype)


def bell_draw_with(key, dims, scale, reach, cuts, heavy, dtype=jnp.bfloat16):
    entries = scale * jax.random.normal(key, dims, jnp.float32)
    if cuts:
        entries = entries * steps_of(key, dims, cuts, -0.22, 0.18)
    return jnp.clip(spiked(entries, jax.random.fold_in(key, 3), *heavy), -reach, reach).astype(dtype)


def setup_inputs(seed: int = 0) -> dict:
    key_list = jax.random.split(jax.random.key(seed), 18)
    inputs = bell_draw(key_list[0], (TOKENS, D), 1.0, 6.0, ((0, 32),))
    gain_mix = jnp.clip(1.0 + 0.18 * jax.random.normal(key_list[1], (D,), jnp.float32), 0.099609375, 1.8984375).astype(jnp.bfloat16)
    gain_mlp = jnp.clip(1.0 + 0.18 * jax.random.normal(key_list[2], (D,), jnp.float32), 0.099609375, 1.8984375).astype(jnp.bfloat16)
    branch_x = bell_draw(key_list[3], (D, LRU), D ** -0.5, 0.125, ((0, 16), (1, 2)))
    branch_y = bell_draw(key_list[4], (D, LRU), D ** -0.5, 0.125, ((0, 16), (1, 2)))
    conv_taps = bell_draw(key_list[5], (TAPS, LRU), TAPS ** -0.5, 3.0, ((1, 32),))
    conv_bias = bell_draw(key_list[6], (LRU,), 0.5, 3.0, ((0, 32),))
    gate_a = bell_draw(key_list[7], (HEADS, BLOCK, BLOCK), BLOCK ** -0.5, 0.375, ((0, 2), (1, 16)))
    bias_a = bell_draw(key_list[8], (LRU,), 1.0, 4.0, ((0, 32),))
    gate_in = bell_draw(key_list[9], (HEADS, BLOCK, BLOCK), BLOCK ** -0.5, 0.375, ((0, 2), (1, 16)))
    bias_in = bell_draw(key_list[10], (LRU,), 1.0, 4.0, ((0, 32),))
    decay_param = jnp.clip(-9.0 + 4.5 * jax.random.uniform(key_list[11], (LRU,), jnp.float32) ** steps_of(key_list[11], (LRU,), ((0, 32),), -0.2, 0.2), -9.0, -4.5).astype(jnp.bfloat16)
    out_proj = bell_draw(key_list[12], (LRU, D), (LRU // 16) ** -0.5, 0.5, ((0, 2), (1, 16)))
    ffn_gate = bell_draw(key_list[13], (D, FF), D ** -0.5, 0.125, ((0, 16), (1, 2)))
    ffn_up = bell_draw(key_list[14], (D, FF), D ** -0.5, 0.125, ((0, 16), (1, 2)))
    ffn_down = bell_draw(key_list[15], (FF, D), (FF // 4) ** -0.5, 0.125, ((0, 2), (1, 16)))
    cotangent = bell_draw_with(key_list[16], (TOKENS, D), 1.0, 6.0, ((0, 32),), (0, 1, 32, 2.75))
    return dict(inputs=inputs, gain_mix=gain_mix, gain_mlp=gain_mlp, branch_x=branch_x, branch_y=branch_y, conv_taps=conv_taps, conv_bias=conv_bias, gate_a=gate_a, bias_a=bias_a, gate_in=gate_in, bias_in=bias_in, decay_param=decay_param, out_proj=out_proj, ffn_gate=ffn_gate, ffn_up=ffn_up, ffn_down=ffn_down, cotangent=cotangent)


@jax.custom_vjp
def low(v):
    return lax.optimization_barrier(v.astype(jnp.bfloat16)).astype(jnp.float32)

@jax.custom_vjp
def low_back(v):
    return v

def low_keep(v):
    return (low(v), None)

def low_pass(kept, grad):
    return (grad,)

def back_keep(v):
    return (v, None)

def back_low(kept, grad):
    return (low(grad),)
low.defvjp(low_keep, low_pass)
low_back.defvjp(back_keep, back_low)
EPSILON = 1e-06

def product(left, right):
    return jnp.dot(left, right, precision=lax.Precision.HIGHEST, preferred_element_type=jnp.float32)

def scale_norm(values, gain):
    return values * lax.rsqrt(lax.optimization_barrier(jnp.mean(values * values, axis=-1, keepdims=True)) + EPSILON) * gain

def convolve(values, taps, bias):
    width = taps.shape[0]
    length = values.shape[0]
    padded = jnp.pad(values, ((width - 1, 0), (0, 0)))
    total = jnp.zeros_like(values) + bias
    for shift_by in range(width):
        total = total + taps[shift_by] * padded[width - 1 - shift_by:width - 1 - shift_by + length]
    return total

def lru_terms(pre_a, pre_i, decay_param, conv_out):
    rate = jax.nn.sigmoid(pre_a)
    entry = jax.nn.sigmoid(pre_i)
    log_decay = -8.0 * jax.nn.softplus(decay_param) * rate
    decay = jnp.exp(log_decay)
    driven = jnp.sqrt(-jnp.expm1(2.0 * log_decay)) * (entry * conv_out)
    return (decay, driven)

def recur(decay, driven):

    def advance(carry, pair):
        carry = pair[0] * carry + pair[1]
        return (carry, carry)
    start = jnp.zeros((decay.shape[1],), jnp.float32)
    _, states = lax.scan(advance, start, (decay, driven))
    return states

def block_gates(rounded, weight, bias):
    length = rounded.shape[0]
    heads = weight.shape[0]
    blocks = rounded.reshape(length, heads, weight.shape[1])
    mixed_in = jnp.einsum('thd,hde->the', blocks, weight, precision=lax.Precision.HIGHEST)
    return mixed_in.reshape(length, heads * weight.shape[2]) + bias

def block_forward(inputs, gain_mix, gain_mlp, branch_x, branch_y, conv_taps, conv_bias, gate_a, bias_a, gate_in, bias_in, decay_param, out_proj, ffn_gate, ffn_up, ffn_down):
    normed = low(scale_norm(inputs, gain_mix))
    pre_x = low_back(product(normed, branch_x))
    pre_y = low_back(product(normed, branch_y))
    gated_y = jax.nn.gelu(pre_y)
    conv_out = convolve(pre_x, conv_taps, conv_bias)
    rounded = low(conv_out)
    pre_a = low_back(block_gates(rounded, gate_a, bias_a))
    pre_i = low_back(block_gates(rounded, gate_in, bias_in))
    decay, driven = lru_terms(pre_a, pre_i, decay_param, conv_out)
    states = recur(decay, driven)
    mixed = low(states * gated_y)
    resid = inputs + low_back(product(mixed, out_proj))
    normed_two = low(scale_norm(resid, gain_mlp))
    gate_pre = low_back(product(normed_two, ffn_gate))
    up_pre = low_back(product(normed_two, ffn_up))
    hidden = low(jax.nn.gelu(gate_pre) * up_pre)
    return resid + low_back(product(hidden, ffn_down))

def reference(inputs, gain_mix, gain_mlp, branch_x, branch_y, conv_taps, conv_bias, gate_a, bias_a, gate_in, bias_in, decay_param, out_proj, ffn_gate, ffn_up, ffn_down, cotangent):
    params = tuple((p.astype(jnp.float32) for p in (gain_mix, gain_mlp, branch_x, branch_y, conv_taps, conv_bias, gate_a, bias_a, gate_in, bias_in, decay_param, out_proj, ffn_gate, ffn_up, ffn_down)))
    sequences = inputs.astype(jnp.float32).reshape(N_DP, SEQ, D)
    upstream = cotangent.astype(jnp.float32).reshape(N_DP, SEQ, D)

    def per_sequence(totals, item):
        outputs, pull = jax.vjp(block_forward, item[0], *params)
        grads = pull(item[1])
        totals = tuple((total + grad for total, grad in zip(totals, grads[1:])))
        return (totals, (outputs.astype(jnp.bfloat16), grads[0]))
    zeros = tuple((jnp.zeros_like(p) for p in params))
    totals, (outputs, grad_rows) = lax.scan(per_sequence, zeros, (sequences, upstream))
    return (outputs.reshape(TOKENS, D), grad_rows.reshape(TOKENS, D), totals[0], totals[1], totals[2], totals[3], totals[4], totals[5], totals[6], totals[7], totals[8], totals[9], totals[10], totals[11], totals[12], totals[13], totals[14])
```

```python
import jax
import jax.numpy as jnp
from jax import lax
from jax.sharding import PartitionSpec as P

EPSILON = 1e-06
F32 = jnp.float32
BF16 = jnp.bfloat16


def contract_last(left, right):
    return lax.dot_general(left, right, (((1,), (1,)), ((), ())), preferred_element_type=F32)


def contract_first(left, right):
    return lax.dot_general(left, right, (((0,), (0,)), ((), ())), preferred_element_type=F32)


def matmul(left, right):
    return jnp.dot(left, right, preferred_element_type=F32)


def scale_norm(values, gain):
    return values * lax.rsqrt(jnp.mean(values * values, axis=-1, keepdims=True) + EPSILON) * gain


def convolve(values, taps, bias):
    width = taps.shape[0]
    length = values.shape[0]
    padded = jnp.pad(values, ((width - 1, 0), (0, 0)))
    total = jnp.zeros_like(values) + bias
    for shift_by in range(width):
        total = (
            total + taps[shift_by] * padded[width - 1 - shift_by : width - 1 - shift_by + length]
        )
    return total


def lru_terms(pre_a, pre_i, decay_param, conv_out):
    rate = jax.nn.sigmoid(pre_a)
    entry = jax.nn.sigmoid(pre_i)
    log_decay = -8.0 * jax.nn.softplus(decay_param) * rate
    decay = jnp.exp(log_decay)
    driven = jnp.sqrt(-jnp.expm1(2.0 * log_decay)) * (entry * conv_out)
    return (decay, driven)


def combine(earlier, later):
    return (earlier[0] * later[0], later[0] * earlier[1] + later[1])


def linear_scan(decay, driven):
    return lax.associative_scan(combine, (decay, driven), axis=0)[1]


class Grid:
    def __init__(self, n):
        self.n = n
        self.nz = n // 4
        index = lax.axis_index("dp")
        self.x = index % 2
        self.y = (index // 2) % 2
        self.z = index // 4
        self.t = lax.axis_index("tensor")

    def place(self, axis):
        return {"x": self.x, "y": self.y, "t": self.t}[axis]

    def swap(self, value, axis):
        if axis == "t":
            return lax.ppermute(value, "tensor", [(0, 1), (1, 0)])
        bit = {"x": 1, "y": 2}[axis]
        return lax.ppermute(value, "dp", [(i, i ^ bit) for i in range(self.n)])

    def shift(self, value, by):
        return lax.ppermute(value, "dp", [(i, (i + 4 * by) % self.n) for i in range(self.n)])

    def pair(self, mine, other, axis):
        here = self.place(axis)
        return jnp.where(here == 0, jnp.stack([mine, other]), jnp.stack([other, mine]))

    def gather(self, value, axis):
        return self.pair(value, self.swap(value, axis), axis)

    def line(self, pieces):
        out = jnp.zeros((self.nz,) + pieces[0].shape, pieces[0].dtype)
        for k, piece in enumerate(pieces):
            out = lax.dynamic_update_index_in_dim(out, piece, (self.z - k) % self.nz, 0)
        return out

    def gather_z(self, value):
        return self.line([value] + [self.shift(value, k) for k in range(1, self.nz)])

    def pick(self, value, axis, dim, other=False):
        here = self.place(axis)
        return lax.dynamic_index_in_dim(value, 1 - here if other else here, dim, keepdims=False)

    def trade_z(self, value):
        take = lambda k: lax.dynamic_index_in_dim(value, (self.z + k) % self.nz, 0, keepdims=False)
        return self.line([take(0)] + [self.shift(take(k), k) for k in range(1, self.nz)])

    def trade(self, value, axis):
        return self.pair(
            self.pick(value, axis, 0), self.swap(self.pick(value, axis, 0, True), axis), axis
        )

    def reduce(self, value, axis, dim):
        got = self.swap(self.pick(value, axis, dim, True).astype(BF16), axis)
        return self.pick(value, axis, dim).astype(F32) + got.astype(F32)

    def reduce_z(self, value):
        take = lambda k: lax.dynamic_index_in_dim(value, (self.z + k) % self.nz, 0, keepdims=False)
        total = take(0).astype(F32)
        for k in range(1, self.nz):
            total = total + self.shift(take(k).astype(BF16), k).astype(F32)
        return total


def local(n):
    def run(
        inputs,
        gain_mix,
        gain_mlp,
        branch_x,
        branch_y,
        conv_taps,
        conv_bias,
        gate_a,
        bias_a,
        gate_in,
        bias_in,
        decay_param,
        out_proj,
        ffn_gate,
        ffn_up,
        ffn_down,
        cotangent,
    ):
        grid = Grid(n)
        nz = grid.nz
        rows_each, width = inputs.shape
        part = branch_x.shape[0]
        half = branch_x.shape[1]
        quarter = half // 2
        heads, gate_rows, block = gate_a.shape
        units = ffn_gate.shape[1] // nz
        split = part // 2

        slim = conv_bias.shape[0]
        vectors = jnp.concatenate(
            [
                conv_taps.reshape(-1),
                conv_bias,
                bias_a,
                bias_in,
                decay_param,
                gain_mix,
                gain_mlp,
            ]
        )
        n_vec = vectors.shape[0]
        packed = jnp.concatenate(
            [
                jnp.transpose(gate_a, (1, 0, 2)).reshape(gate_rows, half),
                jnp.transpose(gate_in, (1, 0, 2)).reshape(gate_rows, half),
                jnp.pad(vectors, (0, half - n_vec))[None],
            ]
        )
        small = grid.gather(grid.gather(grid.gather_z(packed), "y"), "x")
        small = jnp.transpose(small, (2, 1, 0, 3, 4)).reshape(n, -1, half)
        full_gate_a = jnp.transpose(
            small[:, :gate_rows].reshape(n * gate_rows, heads, block), (1, 0, 2)
        )
        full_gate_in = jnp.transpose(
            small[:, gate_rows : 2 * gate_rows].reshape(n * gate_rows, heads, block), (1, 0, 2)
        )
        vecs = small[:, 2 * gate_rows].astype(F32)
        per = jnp.transpose(vecs[:, : 8 * slim].reshape(n, 8, slim), (1, 0, 2)).reshape(8, half)
        full_taps, full_conv_bias = per[:4], per[4]
        full_bias_a, full_bias_in, full_decay = per[5], per[6], per[7]
        full_gain_mix = vecs[:, 8 * slim : 8 * slim + part].reshape(width)
        full_gain_mlp = vecs[:, 8 * slim + part : 8 * slim + 2 * part].reshape(width)

        def mixer_rows(blocks):
            got = grid.gather(grid.gather_z(grid.trade(blocks, "x")), "y")
            return jnp.transpose(got, (1, 0, 2, 3, 4)).reshape(width, -1)

        out_rows = jnp.transpose(out_proj)
        by_x = lambda w: jnp.stack([w[:, :quarter], w[:, quarter:]])
        full_in = mixer_rows(jnp.concatenate([by_x(branch_x), by_x(branch_y)], axis=-1))
        full_out = mixer_rows(by_x(out_rows))

        def ffn_rows(blocks):
            got = grid.trade_z(blocks)
            first = grid.gather(grid.gather(got[:, :split], "y"), "x")
            second = grid.gather(grid.gather(got[:, split:], "x"), "y")
            first = jnp.transpose(first, (2, 1, 0, 3, 4))
            second = jnp.transpose(second, (2, 0, 1, 3, 4))
            return jnp.concatenate([first, second], axis=3).reshape(width, units)

        by_z = lambda w: jnp.transpose(w.reshape(part, nz, units), (1, 0, 2))
        full_down = ffn_rows(jnp.transpose(ffn_down.reshape(nz, units, part), (0, 2, 1)))
        full_gate = ffn_rows(by_z(ffn_gate))
        full_up = ffn_rows(by_z(ffn_up))

        rows = inputs.astype(F32)
        two = grid.gather(grid.gather(inputs, "t"), "x").reshape(4 * rows_each, width)
        length = 2 * rows_each
        normed = scale_norm(two.astype(F32), full_gain_mix).astype(BF16)
        pre = matmul(normed, full_in).reshape(2, length, half)

        def to_channels(value):
            mine = grid.pick(value, "x", 0)
            other = grid.swap(grid.pick(value, "x", 0, True).astype(BF16), "x").astype(value.dtype)
            here = grid.x == 0
            outs = []
            for k in range(value.shape[2] // quarter):
                a = mine[:, k * quarter : (k + 1) * quarter]
                b = other[:, k * quarter : (k + 1) * quarter]
                outs.append(
                    jnp.where(
                        here, jnp.concatenate([a, b], axis=1), jnp.concatenate([b, a], axis=1)
                    )
                )
            return outs

        def to_rows(value):
            halves = jnp.stack([value[:, :quarter], value[:, quarter:]])
            return grid.trade(halves, "x").reshape(2 * length, quarter)

        pre_x, pre_y = to_channels(pre)
        gated_y, gelu_pull = jax.vjp(jax.nn.gelu, pre_y)
        conv_out, conv_pull = jax.vjp(convolve, pre_x, full_taps, full_conv_bias)
        rounded = conv_out.astype(BF16).reshape(length, heads, block)
        pre_a = (
            jnp.einsum("thd,hde->the", rounded, full_gate_a, preferred_element_type=F32).reshape(
                length, half
            )
            + full_bias_a
        )
        pre_i = (
            jnp.einsum("thd,hde->the", rounded, full_gate_in, preferred_element_type=F32).reshape(
                length, half
            )
            + full_bias_in
        )
        (decay, driven), lru_pull = jax.vjp(lru_terms, pre_a, pre_i, full_decay, conv_out)
        states = linear_scan(decay, driven)
        mixed = to_rows((states * gated_y).astype(BF16))
        branch_out = contract_last(mixed, full_out).reshape(2, 2, rows_each, width)
        branch_out = grid.reduce(grid.reduce(branch_out, "t", 1), "x", 0)
        resid = rows + branch_out

        normed_two_rows, norm_two_pull = jax.vjp(scale_norm, resid, full_gain_mlp)
        to_line = lambda v: grid.gather(grid.gather_z(v), "t")
        tokens = nz * length
        normed_two = to_line(normed_two_rows.astype(BF16)).reshape(tokens, width)
        upstream = to_line(cotangent).reshape(tokens, width)

        def from_line(partial):
            partial = partial.reshape(2, nz, rows_each, width)
            return grid.reduce_z(grid.reduce(partial, "t", 0))

        grad_hidden = matmul(upstream, full_down)
        gate_pre = matmul(normed_two, full_gate)
        up_pre = matmul(normed_two, full_up)
        gate_act, gate_pull = jax.vjp(jax.nn.gelu, gate_pre)
        hidden = (gate_act * up_pre).astype(BF16)
        grad_gate_pre = gate_pull(grad_hidden * up_pre)[0].astype(BF16)
        grad_up_pre = (grad_hidden * gate_act).astype(BF16)
        grad_normed_two = from_line(
            contract_last(grad_gate_pre, full_gate) + contract_last(grad_up_pre, full_up)
        )
        result = (resid + from_line(contract_last(hidden, full_down))).astype(BF16)

        def ffn_reduce(grad):
            grad = grad.reshape(nz, 2, 2, part, units)
            first = grid.reduce(grid.reduce(grad[:, :, :, :split], "x", 2), "y", 1)
            second = grid.reduce(grid.reduce(grad[:, :, :, split:], "y", 1), "x", 1)
            both = jnp.concatenate([first, second], axis=1).astype(BF16)
            return grid.trade_z(both)

        wide = lambda g: jnp.transpose(g, (1, 0, 2)).reshape(part, nz * units).astype(F32)
        grad_gate = wide(ffn_reduce(contract_first(normed_two, grad_gate_pre)))
        grad_up = wide(ffn_reduce(contract_first(normed_two, grad_up_pre)))
        grad_down = ffn_reduce(contract_first(upstream, hidden))
        grad_down = jnp.transpose(grad_down, (0, 2, 1)).reshape(nz * units, part).astype(F32)

        grad_resid_norm, _ = norm_two_pull(grad_normed_two)
        grad_resid = cotangent.astype(F32) + grad_resid_norm
        back = grid.gather(grid.gather(grad_resid.astype(BF16), "t"), "x").reshape(-1, width)
        (grad_mixed,) = to_channels(matmul(back, full_out).reshape(2, length, quarter))
        grad_out = contract_first(back, mixed)
        grad_states = grad_mixed * gated_y
        grad_pre_y = gelu_pull(grad_mixed * states)[0].astype(BF16)
        next_decay = jnp.concatenate([decay[1:], jnp.zeros_like(decay[:1])], axis=0)
        grad_driven = jnp.flip(linear_scan(jnp.flip(next_decay, 0), jnp.flip(grad_states, 0)), 0)
        prior_states = jnp.concatenate([jnp.zeros_like(states[:1]), states[:-1]], axis=0)
        grad_decay = grad_driven * prior_states
        grad_pre_a, grad_pre_i, grad_decay_raw, grad_conv_direct = lru_pull(
            (grad_decay, grad_driven)
        )
        rounded_grad_a = grad_pre_a.astype(BF16)
        rounded_grad_i = grad_pre_i.astype(BF16)
        blocks_a = rounded_grad_a.reshape(length, heads, block)
        blocks_i = rounded_grad_i.reshape(length, heads, block)
        grad_rounded = jnp.einsum(
            "the,hde->thd", blocks_a, full_gate_a, preferred_element_type=F32
        ) + jnp.einsum("the,hde->thd", blocks_i, full_gate_in, preferred_element_type=F32)
        grad_gate_a = jnp.einsum("thd,the->dhe", rounded, blocks_a, preferred_element_type=F32)
        grad_gate_in = jnp.einsum("thd,the->dhe", rounded, blocks_i, preferred_element_type=F32)
        grad_bias_a = jnp.sum(rounded_grad_a.astype(F32), axis=0)
        grad_bias_in = jnp.sum(rounded_grad_i.astype(F32), axis=0)
        grad_conv = grad_conv_direct + grad_rounded.reshape(length, half)
        grad_pre_x, grad_taps, grad_conv_bias = conv_pull(grad_conv)
        grad_in_rows = jnp.concatenate(
            [to_rows(grad_pre_x.astype(BF16)), to_rows(grad_pre_y)], axis=1
        )
        grad_in = contract_first(normed, grad_in_rows)

        def mixer_reduce(grad):
            grad = grad.reshape(nz, 2, 2, part, -1)
            return grid.trade(grid.reduce_z(grid.reduce(grad, "y", 1)).astype(BF16), "x")

        grad_out = mixer_reduce(grad_out)
        grad_out = jnp.transpose(grad_out, (0, 2, 1)).reshape(half, part).astype(F32)
        grad_in = mixer_reduce(grad_in).astype(F32)
        join = lambda g: jnp.concatenate([g[0], g[1]], axis=1)
        grad_branch_x = join(grad_in[:, :, :quarter])
        grad_branch_y = join(grad_in[:, :, quarter:])

        vec = jnp.concatenate(
            [
                grad_taps,
                grad_conv_bias[None],
                grad_bias_a[None],
                grad_bias_in[None],
                grad_decay_raw[None],
            ]
        )
        vec = jnp.transpose(vec.reshape(8, n, slim), (1, 0, 2)).reshape(n, 1, 8 * slim)
        grad_small = jnp.concatenate(
            [
                grad_gate_a.reshape(n, gate_rows, half),
                grad_gate_in.reshape(n, gate_rows, half),
                jnp.pad(vec, ((0, 0), (0, 0), (0, half - 8 * slim))),
            ],
            axis=1,
        ).reshape(nz, 2, 2, 2 * gate_rows + 1, half)
        grad_small = grid.reduce_z(grid.reduce(grid.reduce(grad_small, "x", 2), "y", 1))
        unpack = lambda g: jnp.transpose(g.reshape(gate_rows, heads, block), (1, 0, 2))
        vec = grad_small[2 * gate_rows, : 8 * slim].reshape(8, slim)

        grad_normed = matmul_t(grad_in_rows, full_in).reshape(2, 2, rows_each, width)
        grad_normed = grid.reduce(grid.reduce(grad_normed, "t", 1), "x", 0)
        _, norm_pull = jax.vjp(scale_norm, rows, full_gain_mix)
        grad_rows, _ = norm_pull(grad_normed)
        grad_inputs = grad_resid + grad_rows

        gains = jnp.stack(
            [
                jnp.sum(
                    branch_x.astype(F32) * grad_branch_x + branch_y.astype(F32) * grad_branch_y,
                    axis=1,
                )
                / gain_mix.astype(F32),
                jnp.sum(
                    ffn_gate.astype(F32) * grad_gate + ffn_up.astype(F32) * grad_up,
                    axis=1,
                )
                / gain_mlp.astype(F32),
            ]
        )
        gains = gains + grid.swap(gains, "t")
        gains = lax.dynamic_index_in_dim(gains.reshape(2, 2, split), grid.t, 1, keepdims=False)
        return (
            result,
            grad_inputs,
            gains[0],
            gains[1],
            grad_branch_x,
            grad_branch_y,
            vec[:4],
            vec[4],
            unpack(grad_small[:gate_rows]),
            vec[5],
            unpack(grad_small[gate_rows : 2 * gate_rows]),
            vec[6],
            vec[7],
            grad_out,
            grad_gate,
            grad_up,
            grad_down,
        )

    return run


def matmul_t(left, right):
    return contract_last(left, right)


def solution(mesh):
    in_specs = (
        P(("dp", "tensor"), None),
        P("dp"),
        P("dp"),
        P("dp", "tensor"),
        P("dp", "tensor"),
        P(None, ("tensor", "dp")),
        P(("tensor", "dp")),
        P("tensor", "dp", None),
        P(("tensor", "dp")),
        P("tensor", "dp", None),
        P(("tensor", "dp")),
        P(("tensor", "dp")),
        P("tensor", "dp"),
        P("dp", "tensor"),
        P("dp", "tensor"),
        P("tensor", "dp"),
        P(("dp", "tensor"), None),
    )
    out_specs = (
        P(("dp", "tensor"), None),
        P(("dp", "tensor"), None),
        P(("dp", "tensor")),
        P(("dp", "tensor")),
        P("dp", "tensor"),
        P("dp", "tensor"),
        P(None, ("tensor", "dp")),
        P(("tensor", "dp")),
        P("tensor", "dp", None),
        P(("tensor", "dp")),
        P("tensor", "dp", None),
        P(("tensor", "dp")),
        P(("tensor", "dp")),
        P("tensor", "dp"),
        P("dp", "tensor"),
        P("dp", "tensor"),
        P("tensor", "dp"),
    )
    return jax.shard_map(
        local(mesh.shape["dp"]),
        mesh=mesh,
        in_specs=in_specs,
        out_specs=out_specs,
        check_vma=False,
    )
```

```python
import math

import jax
import jax.numpy as jnp
from jax import lax
from jax.experimental import pallas as pl
from jax.experimental.pallas import tpu as pltpu
from jax.sharding import PartitionSpec as P

EPSILON = 1e-06
F32 = jnp.float32
BF16 = jnp.bfloat16


def matmul(left, right):
    return jnp.dot(left, right, preferred_element_type=F32)


def contract_last(left, right):
    return lax.dot_general(left, right, (((1,), (1,)), ((), ())), preferred_element_type=F32)


def contract_first(left, right):
    return lax.dot_general(left, right, (((0,), (0,)), ((), ())), preferred_element_type=F32)


def scale_norm(values, gain):
    return values * lax.rsqrt(jnp.mean(values * values, axis=-1, keepdims=True) + EPSILON) * gain


def down(value, by, fill):
    row = lax.broadcasted_iota(jnp.int32, value.shape, 0)
    return jnp.where(row < by, fill, pltpu.roll(value, by, 0))


def up(value, by, fill):
    length = value.shape[0]
    row = lax.broadcasted_iota(jnp.int32, value.shape, 0)
    return jnp.where(row >= length - by, fill, pltpu.roll(value, length - by, 0))


def scan(shift, decay, driven):
    by = 1
    while by < decay.shape[0]:
        driven = driven + decay * shift(driven, by, 0.0)
        if 2 * by < decay.shape[0]:
            decay = decay * shift(decay, by, 1.0)
        by *= 2
    return driven


def minus_expm1(u):
    series = 1.0 + u * (1 / 7)
    for k in (6, 5, 4, 3, 2):
        series = 1.0 + u * (1 / k) * series
    return jnp.where(u > -0.25, -u * series, 1.0 - jnp.exp(u))


def gelu_parts(v):
    inner = 0.7978845608 * (v + 0.044715 * v * v * v)
    tanh = jnp.tanh(inner)
    value = 0.5 * v * (1.0 + tanh)
    slope = 0.5 * (1.0 + tanh) + 0.5 * v * (1.0 - tanh * tanh) * 0.7978845608 * (
        1.0 + 3 * 0.044715 * v * v
    )
    return value, slope


def mixer_forward(px, py, ga, gi, vec, mixed, states, conv, rate, entry):
    taps = vec[...]
    value = px[...]
    total = taps[4:5] + taps[0:1] * value
    for k in range(1, 4):
        total = total + taps[k : k + 1] * down(value, k, 0.0)
    rounded = total.astype(BF16)
    r = jax.nn.sigmoid(matmul(rounded, ga[0]) + taps[5:6])
    e = jax.nn.sigmoid(matmul(rounded, gi[0]) + taps[6:7])
    log_decay = -8.0 * taps[7:8] * r
    driven = jnp.sqrt(minus_expm1(2.0 * log_decay)) * (e * total)
    s = scan(down, jnp.exp(log_decay), driven)
    mixed[...] = (s * gelu_parts(py[...])[0]).astype(BF16)
    states[...] = s
    conv[...] = total
    rate[...] = r
    entry[...] = e


def mixer_backward(gm, px, py, ga, gi, vec, states, conv, rate, entry, gpx, gga, ggi, gvec):
    taps = vec[...]
    s, total, r, e, grad = states[...], conv[...], rate[...], entry[...], gm[...]
    gated = gelu_parts(py[...])[0]
    log_decay = -8.0 * taps[7:8] * r
    decay = jnp.exp(log_decay)
    root = jnp.sqrt(minus_expm1(2.0 * log_decay))
    grad_driven = scan(up, up(decay, 1, 0.0), grad * gated)
    grad_decay = grad_driven * down(s, 1, 0.0)
    grad_root = grad_driven * (e * total)
    grad_log = grad_decay * decay - grad_root * (decay * decay) / root
    grad_rate = grad_log * (-8.0 * taps[7:8])
    grad_entry = grad_driven * root * total
    ra = (grad_rate * r * (1.0 - r)).astype(BF16)
    ri = (grad_entry * e * (1.0 - e)).astype(BF16)
    rounded = total.astype(BF16)
    gga[...] = contract_first(rounded, ra)
    ggi[...] = contract_first(rounded, ri)
    grad_conv = (
        grad_driven * root * e + contract_last(ra, ga[0]) + contract_last(ri, gi[0])
    )
    value = px[...]
    back = taps[0:1] * grad_conv
    sums = [jnp.sum(grad_conv * value, axis=0, keepdims=True)]
    for k in range(1, 4):
        back = back + taps[k : k + 1] * up(grad_conv, k, 0.0)
        sums.append(jnp.sum(grad_conv * down(value, k, 0.0), axis=0, keepdims=True))
    gpx[...] = back.astype(BF16)
    sums.append(jnp.sum(grad_conv, axis=0, keepdims=True))
    sums.append(jnp.sum(ra.astype(F32), axis=0, keepdims=True))
    sums.append(jnp.sum(ri.astype(F32), axis=0, keepdims=True))
    sums.append(jnp.sum(grad_log * (-8.0 * r), axis=0, keepdims=True))
    gvec[...] = jnp.concatenate(sums, axis=0)


def by_head(kernel, heads, length, block, kinds, outs):
    spec = {
        "r": pl.BlockSpec((length, block), lambda h: (0, h)),
        "g": pl.BlockSpec((1, block, block), lambda h: (h, 0, 0)),
        "v": pl.BlockSpec((8, block), lambda h: (0, h)),
        "w": pl.BlockSpec((block, block), lambda h: (0, h)),
    }
    sizes = {"r": (length, heads * block), "v": (8, heads * block), "w": (block, heads * block)}
    return pl.pallas_call(
        kernel,
        grid=(heads,),
        in_specs=[spec[k] for k in kinds],
        out_specs=[spec[k] for k, _ in outs],
        out_shape=[jax.ShapeDtypeStruct(sizes[k], d) for k, d in outs],
        compiler_params=pltpu.CompilerParams(vmem_limit_bytes=32 * 1024 * 1024),
    )


def scalar(value):
    return jnp.asarray(value, jnp.int32).reshape(1)


def whole(shape):
    return pl.BlockSpec(shape, lambda *_: (0,) * len(shape))


def params(mib):
    return pltpu.CompilerParams(vmem_limit_bytes=mib * 1024 * 1024)


def cut(values, z, nz):
    part, columns = values[0].shape
    units = columns // nz
    n = len(values)

    def kernel(where, *refs):
        for here in range(nz):

            @pl.when(where[0] == here)
            def _():
                for k in range(nz):
                    first = (here + k) % nz * units
                    for w in range(n):
                        refs[n + k][w] = refs[w][:, first : first + units]

    return pl.pallas_call(
        kernel,
        in_specs=[pl.BlockSpec(memory_space=pltpu.SMEM)] + [whole((part, columns))] * n,
        out_specs=[whole((n, part, units))] * nz,
        out_shape=[jax.ShapeDtypeStruct((n, part, units), values[0].dtype)] * nz,
        compiler_params=params(40),
    )(scalar(z), *values)


def line_up(pieces, z):
    nz = len(pieces)
    n, *rest = pieces[0].shape

    def kernel(where, *refs):
        for k in range(nz):
            to = lax.rem(where[0] - k + nz, nz)
            for w in range(n):
                refs[-1][w, to] = refs[k][w]

    return pl.pallas_call(
        kernel,
        in_specs=[pl.BlockSpec(memory_space=pltpu.SMEM)] + [whole((n, *rest))] * nz,
        out_specs=whole((n, nz, *rest)),
        out_shape=jax.ShapeDtypeStruct((n, nz, *rest), pieces[0].dtype),
        compiler_params=params(40),
    )(scalar(z), *pieces)


def norm_rows(here, across, gain, t):
    rows, width = here[0].shape

    def kernel(where, gain, *refs):
        for s in range(2):
            for other in range(2):
                value = refs[2 * s + other][...].astype(F32)
                scale = lax.rsqrt(jnp.mean(value * value, axis=-1, keepdims=True) + EPSILON)
                place = 1 - where[0] if other else where[0]
                first = pl.multiple_of((2 * s + place) * rows, rows)
                refs[4][pl.ds(first, rows), :] = (value * scale * gain[...]).astype(BF16)

    return pl.pallas_call(
        kernel,
        in_specs=[pl.BlockSpec(memory_space=pltpu.SMEM), whole((1, width))]
        + [whole((rows, width))] * 4,
        out_specs=whole((4 * rows, width)),
        out_shape=jax.ShapeDtypeStruct((4 * rows, width), BF16),
        compiler_params=params(32),
    )(scalar(t), gain.reshape(1, width), *here, *across)


def join(pieces, weights, z):
    nz = len(pieces)
    n, part, units = pieces[0].shape
    shape = weights[0].shape

    def kernel(where, *refs):
        for w in range(n):
            out, sums = refs[n + nz + w], refs[2 * n + nz + w]
            for here in range(nz):

                @pl.when(where[0] == here)
                def _():
                    for k in range(nz):
                        first = (here - k) % nz * units
                        out[:, first : first + units] = refs[n + k][w].astype(F32)

            sums[...] = jnp.sum(out[...] * refs[w][...].astype(F32), axis=1, keepdims=True)

    outs = pl.pallas_call(
        kernel,
        in_specs=[pl.BlockSpec(memory_space=pltpu.SMEM)]
        + [whole(shape)] * n
        + [whole((n, part, units))] * nz,
        out_specs=[whole(shape)] * n + [whole((part, 1))] * n,
        out_shape=[jax.ShapeDtypeStruct(shape, F32)] * n
        + [jax.ShapeDtypeStruct((part, 1), F32)] * n,
        compiler_params=params(48),
    )(scalar(z), *weights, *pieces)
    return outs[:n], outs[n:]


def reorder(value, nz, back):
    rows, width = value.shape
    part = width // (4 * nz)

    def kernel(source, out):
        for k in range(4):
            for z in range(nz):
                natural, own = (z * 4 + k) * part, (k * nz + z) * part
                to, of = (natural, own) if back else (own, natural)
                out[:, to : to + part] = source[:, of : of + part]

    return pl.pallas_call(
        kernel,
        in_specs=[whole(value.shape)],
        out_specs=whole(value.shape),
        out_shape=jax.ShapeDtypeStruct(value.shape, value.dtype),
        compiler_params=params(32),
    )(value)


TILE = 256
GATE, UP, DOWN = range(3)


def rows_of(width):
    return pl.BlockSpec((TILE, width), lambda i: (i, 0))


def weight_of(weights, which):
    corners, _, *rest = weights.shape
    return pl.BlockSpec((corners, 1, *rest), lambda i: (0, which, 0, 0, 0))


def flat(ref):
    return ref[...].reshape(-1, ref.shape[-1])


def ffn_down_back(act, weights):
    tokens, width = act.shape
    units = weights.shape[-1]

    def kernel(act, down, out):
        out[...] = matmul(act[...], flat(down))

    return pl.pallas_call(
        kernel,
        grid=(tokens // TILE,),
        in_specs=[rows_of(width), weight_of(weights, DOWN)],
        out_specs=rows_of(units),
        out_shape=jax.ShapeDtypeStruct((tokens, units), F32),
        compiler_params=params(48),
    )(act, weights)


def ffn_middle(act, weights, grad_hidden):
    tokens, width = act.shape
    units = weights.shape[-1]

    def kernel(act, grad, gate, up, hidden, grads):
        value = act[...]
        gate_pre = matmul(value, flat(gate))
        up_pre = matmul(value, flat(up))
        active, slope = gelu_parts(gate_pre)
        hidden[...] = (active * up_pre).astype(BF16)
        grads[0] = (slope * (grad[...] * up_pre)).astype(BF16)
        grads[1] = (grad[...] * active).astype(BF16)

    return pl.pallas_call(
        kernel,
        grid=(tokens // TILE,),
        in_specs=[
            rows_of(width),
            rows_of(units),
            weight_of(weights, GATE),
            weight_of(weights, UP),
        ],
        out_specs=[rows_of(units), pl.BlockSpec((2, TILE, units), lambda i: (0, i, 0))],
        out_shape=[
            jax.ShapeDtypeStruct((tokens, units), BF16),
            jax.ShapeDtypeStruct((2, tokens, units), BF16),
        ],
        compiler_params=params(56),
    )(act, grad_hidden, weights, weights)


def ffn_collect(acts, weights, which, dtype):
    n, tokens, units = acts.shape
    width = weights.shape[0] * weights.shape[2] * weights.shape[3]

    def kernel(acts, *refs):
        total = contract_last(acts[0], flat(refs[0]))
        for p in range(1, n):
            total = total + contract_last(acts[p], flat(refs[p]))
        refs[n][...] = total.astype(dtype)

    return pl.pallas_call(
        kernel,
        grid=(tokens // TILE,),
        in_specs=[pl.BlockSpec((n, TILE, units), lambda i: (0, i, 0))]
        + [weight_of(weights, w) for w in which],
        out_specs=rows_of(width),
        out_shape=jax.ShapeDtypeStruct((tokens, width), dtype),
        compiler_params=params(56),
    )(acts, *[weights] * n)


def weight_grad(acts, grads, lead, tail, dtype, n=None, at=0, into=None):
    tokens, width = acts[0].shape
    m, _, columns = grads[0].shape
    n = n or m
    p = len(acts)
    shape = lead + tail
    block = math.prod(shape)
    at_once = math.lcm(block, 128) // block
    ones = (0,) * len(lead), (0,) * (len(tail) + 1)
    full = (width // block, *lead, n, *tail, columns)

    def kernel(*refs):
        total = contract_first(refs[0][...], refs[p][0])
        for k in range(1, p):
            total = total + contract_first(refs[k][...], refs[p + k][0])
        refs[-1][...] = total.reshape(refs[-1].shape).astype(dtype)

    return pl.pallas_call(
        kernel,
        grid=(m, width // block // at_once),
        in_specs=[pl.BlockSpec((tokens, block * at_once), lambda w, i: (0, i))] * p
        + [pl.BlockSpec((1, tokens, columns), lambda w, i: (w, 0, 0))] * p
        + ([] if into is None else [pl.BlockSpec(memory_space=pl.ANY)]),
        out_specs=pl.BlockSpec(
            (at_once, *lead, 1, *tail, columns), lambda w, i: (i, *ones[0], w + at, *ones[1])
        ),
        out_shape=jax.ShapeDtypeStruct(full, dtype),
        input_output_aliases={} if into is None else {2 * p: 0},
        compiler_params=params(48),
    )(*acts, *grads, *([] if into is None else [into]))


def after(value, *deps):
    return lax.optimization_barrier((value,) + deps)[0]


class Grid:
    def __init__(self, n):
        self.n = n
        self.nz = n // 4
        index = lax.axis_index("dp")
        self.x = index % 2
        self.y = (index // 2) % 2
        self.z = index // 4
        self.t = lax.axis_index("tensor")
        self.corners = [[4 * z + k for k in range(4)] for z in range(self.nz)]
        self.planes = [[4 * z + 2 * y + x for z in range(self.nz) for y in range(2)] for x in range(2)]

    def place(self, axis):
        return {"x": self.x, "y": self.y, "t": self.t}[axis]

    def swap(self, value, axis):
        if axis == "t":
            return lax.ppermute(value, "tensor", [(0, 1), (1, 0)])
        bit = {"x": 1, "y": 2}[axis]
        return lax.ppermute(value, "dp", [(i, i ^ bit) for i in range(self.n)])

    def shift(self, value, by):
        return lax.ppermute(value, "dp", [(i, (i + 4 * by) % self.n) for i in range(self.n)])

    def pair(self, mine, other, axis):
        here = self.place(axis)
        return jnp.where(here == 0, jnp.stack([mine, other]), jnp.stack([other, mine]))

    def pick(self, value, axis, dim, other=False):
        here = self.place(axis)
        return lax.dynamic_index_in_dim(value, 1 - here if other else here, dim, keepdims=False)

    def shifts(self, pieces):
        return [pieces[0]] + [self.shift(p, k) for k, p in enumerate(pieces) if k]

    def trade(self, value, axis):
        return self.pair(
            self.pick(value, axis, 0), self.swap(self.pick(value, axis, 0, True), axis), axis
        )

    def reduce(self, value, axis, dim):
        got = self.swap(self.pick(value, axis, dim, True).astype(BF16), axis)
        return self.pick(value, axis, dim).astype(F32) + got.astype(F32)

    def reduce_z(self, value):
        take = lambda k: lax.dynamic_index_in_dim(value, (self.z + k) % self.nz, 0, keepdims=False)
        total = take(0).astype(F32)
        for k in range(1, self.nz):
            total = total + self.shift(take(k).astype(BF16), k).astype(F32)
        return total


def local(n):
    def run(
        inputs,
        gain_mix,
        gain_mlp,
        branch_x,
        branch_y,
        conv_taps,
        conv_bias,
        gate_a,
        bias_a,
        gate_in,
        bias_in,
        decay_param,
        out_proj,
        ffn_gate,
        ffn_up,
        ffn_down,
        cotangent,
    ):
        grid = Grid(n)
        nz = grid.nz
        rows_each, width = inputs.shape
        part, half = branch_x.shape
        quarter = half // 2
        heads, gate_rows, block = gate_a.shape
        units = ffn_gate.shape[1] // nz
        split = part // 2
        run_len = nz * part
        length = 2 * rows_each
        slim = conv_bias.shape[0]
        here_x = grid.x == 0

        vectors = jnp.concatenate(
            [conv_taps.reshape(-1), conv_bias, bias_a, bias_in, decay_param, gain_mix, gain_mlp]
        )
        pad_rows = -(2 * gate_rows + 1) % 16 + 1
        packed = jnp.concatenate(
            [
                jnp.transpose(gate_a, (1, 0, 2)).reshape(gate_rows, half),
                jnp.transpose(gate_in, (1, 0, 2)).reshape(gate_rows, half),
                jnp.pad(vectors[None], ((0, pad_rows - 1), (0, half - vectors.shape[0]))),
            ]
        )
        early = grid.shifts([packed[None]] * nz)
        small = line_up(early, grid.z)[0]
        small = grid.pair(small, grid.swap(small, "y"), "y")
        small = grid.pair(small, grid.swap(small, "x"), "x")
        small = jnp.transpose(small, (2, 1, 0, 3, 4)).reshape(n, -1, half)
        gates = small[:, : 2 * gate_rows].reshape(n, 2, gate_rows, heads, block)
        gates = jnp.transpose(gates, (1, 3, 0, 2, 4)).reshape(2, heads, n * gate_rows, block)
        full_gate_a, full_gate_in = gates[0], gates[1]
        vecs = small[:, 2 * gate_rows].astype(F32)
        per = jnp.transpose(vecs[:, : 8 * slim].reshape(n, 8, slim), (1, 0, 2)).reshape(8, half)
        decay_row = per[7:8]
        per = jnp.concatenate([per[:7], jax.nn.softplus(decay_row)])
        full_gain_mix = vecs[:, 8 * slim : 8 * slim + part].reshape(width)
        full_gain_mlp = vecs[:, 8 * slim + part : 8 * slim + 2 * part].reshape(width)

        by_x = lambda w: jnp.stack([w[:, :quarter], w[:, quarter:]])
        mine = jnp.concatenate([by_x(branch_x), by_x(branch_y)], axis=-1)
        mine = grid.trade(mine, "x").reshape(2 * part, -1)
        full_in = lax.all_gather(mine, "dp", axis=0, tiled=True, axis_index_groups=grid.planes)
        across = grid.swap(after(inputs, mine), "x")

        normed = norm_rows(
            (inputs, grid.swap(inputs, "t")), (across, grid.swap(across, "t")), full_gain_mix, grid.t
        )

        down_rows = jnp.transpose(ffn_down)
        slices = cut((ffn_gate, ffn_up, down_rows), grid.z, nz)
        slices = grid.shifts(slices)
        out_mine = grid.trade(by_x(jnp.transpose(out_proj)), "x").reshape(1, 2 * part, -1)
        out_line = grid.shifts([after(out_mine, slices[1])] * nz)
        weights = lax.all_gather(
            after(line_up(slices, grid.z)[None], full_in, small),
            "dp",
            axis=0,
            tiled=True,
            axis_index_groups=grid.corners,
        )

        def to_line(value, *deps):
            value = after(reorder(value, nz, False), *deps)
            return grid.shifts([value] * nz)

        rows = inputs.astype(F32)
        cot_line = to_line(cotangent, slices[1])
        pre = matmul(normed, full_in).reshape(2, length, 2 * quarter)

        def whole_half(mine, other):
            return jnp.where(
                here_x, jnp.concatenate([mine, other], 1), jnp.concatenate([other, mine], 1)
            )

        def to_rows(value):
            low, high = value[:, :quarter], value[:, quarter:]
            away = grid.swap(jnp.where(here_x, high, low), "x")
            return jnp.concatenate([jnp.where(here_x, low, high), away])

        got = grid.swap(pre[1].astype(BF16), "x").astype(F32)
        got = after(got, cot_line[1])
        out_here = line_up(after(out_line, got), grid.z)[0]
        full_out = grid.pair(out_here, grid.swap(out_here, "y"), "y")
        full_out = jnp.swapaxes(full_out, 0, 1).reshape(width, -1)
        pre_x = whole_half(pre[0, :, :quarter], got[:, :quarter])
        pre_y = whole_half(pre[0, :, quarter:], got[:, quarter:])
        mixed, states, conv, rate, entry = by_head(
            mixer_forward, heads, length, block, "rrggv", [("r", BF16)] + [("r", F32)] * 4
        )(pre_x, pre_y, full_gate_a, full_gate_in, per)
        mixed = after(to_rows(mixed), cot_line[2])
        branch_out = contract_last(mixed, full_out).reshape(2, 2, rows_each, width)
        branch_out = grid.reduce(branch_out, "t", 1)
        branch_out = branch_out[0] + grid.swap(branch_out[1].astype(BF16), "x").astype(F32)
        resid = after(rows + branch_out, *cot_line)

        normed_two_rows, norm_two_pull = jax.vjp(scale_norm, resid, full_gain_mlp)
        def from_line(acts, which, *deps):
            other = ffn_collect(acts[1], weights, which, BF16)
            other = grid.swap(other, "t")
            value = ffn_collect(acts[0], weights, which, F32) + other.astype(F32)
            value = after(value.reshape(nz, rows_each, width), *deps)
            away = [value[k].astype(BF16) for k in range(1, nz)]
            return away, [value[0]] + [grid.shift(v, -1 - k) for k, v in enumerate(away)]

        def total(got):
            return reorder(sum(g.astype(F32) for g in got), nz, True)

        def both_t(line):
            rows = jnp.concatenate(line)
            return rows, grid.swap(rows, "t")

        upstream = both_t(cot_line)
        grad_hidden = [ffn_down_back(u, weights) for u in upstream]
        normed_two = both_t(to_line(normed_two_rows.astype(BF16)))
        hidden, grad_pre = zip(
            *[ffn_middle(a, weights, g) for a, g in zip(normed_two, grad_hidden)]
        )
        hidden = [h[None] for h in hidden]
        sent, got_result = from_line(hidden, (DOWN,))
        upstream, normed_two = after((upstream, normed_two), *sent)
        grad_ffn = weight_grad(normed_two, grad_pre, (), (nz, part), BF16, 3)
        grad_ffn = weight_grad(upstream, hidden, (), (nz, part), BF16, 3, 2, grad_ffn)
        grad_pre = after(grad_pre, grad_ffn, got_result[1])
        sent, got_two = from_line(grad_pre, (GATE, UP))

        def ffn_send(value, *deps):
            value = after(value, *deps)
            take = lambda k: lax.dynamic_index_in_dim(value, (grid.z + k) % nz, 1, keepdims=False)
            return grid.shifts([take(k) for k in range(nz)])

        grad_ffn = lax.psum_scatter(
            grad_ffn, "dp", scatter_dimension=0, tiled=True, axis_index_groups=grid.corners
        )
        grad_normed_two = total(after(got_two, *got_result[1:]))
        grad_ffn = ffn_send(grad_ffn[0], got_two[1])

        grad_resid_norm, _ = norm_two_pull(grad_normed_two)
        grad_resid = cotangent.astype(F32) + grad_resid_norm
        back = grad_resid.astype(BF16)
        back = jnp.stack([back, grid.swap(back, "x")])
        back = jnp.swapaxes(grid.pair(back, grid.swap(back, "t"), "t"), 0, 1)
        back = back.reshape(2 * length, width)
        grad_mixed = matmul(back, full_out).reshape(2, length, quarter)
        grad_mixed = whole_half(
            grad_mixed[0], grid.swap(grad_mixed[1].astype(BF16), "x").astype(F32)
        )
        grad_mixed = after(grad_mixed, grad_ffn[1])
        grad_pre_y = gelu_parts(pre_y)[1] * (grad_mixed * states)
        grad_y_rows = to_rows(grad_pre_y.astype(BF16))

        def mixer_reduce(grad):
            grad = grad.reshape(nz, 2, 2, part, -1)
            away = grid.swap(grid.pick(grad, "y", 1, True).astype(BF16), "y")
            return grid.pick(grad, "y", 1), away

        def mixer_send(value, *deps):
            here, away = after(value, *deps)
            value = here + away.astype(F32)
            take = lambda k: lax.dynamic_index_in_dim(value, (grid.z + k) % nz, 0, keepdims=False)
            got = [take(0)] + [grid.shift(take(k).astype(BF16), k) for k in range(1, nz)]
            return got

        def mixer_finish(got):
            return grid.trade(got, "x")

        grad_oy = weight_grad([back], [mixed[None]], (2,), (2, part), BF16, 2)
        grad_oy = weight_grad([normed], [grad_y_rows[None]], (2,), (2, part), BF16, 2, 1, grad_oy)
        grad_oy = lax.psum_scatter(
            grad_oy.reshape(2 * nz, 2, 2, part, quarter),
            "dp",
            scatter_dimension=0,
            tiled=True,
            axis_index_groups=grid.planes,
        )[0]
        grad_pre_x, grad_gate_a, grad_gate_in, grad_vec = by_head(
            mixer_backward,
            heads,
            length,
            block,
            "rrrggvrrrr",
            [("r", BF16), ("w", F32), ("w", F32), ("v", F32)],
        )(grad_mixed, pre_x, pre_y, full_gate_a, full_gate_in, per, states, conv, rate, entry)
        grad_vec = jnp.concatenate([grad_vec[:7], grad_vec[7:] * jax.nn.sigmoid(decay_row)])
        grad_x_rows = to_rows(grad_pre_x)
        grad_x = mixer_reduce(weight_grad([normed], [grad_x_rows[None]], (), (4, part), F32))
        grad_x = mixer_send(grad_x, *grad_ffn[1:])
        grad_in_rows = jnp.concatenate([grad_x_rows, grad_y_rows], axis=1)

        result = (resid + total(got_result)).astype(BF16)
        (grad_gate, grad_up, grad_down), sums = join(
            after(grad_ffn, *grad_x[1:]), (ffn_gate, ffn_up, down_rows), grid.z
        )
        grad_down = jnp.transpose(grad_down)
        grad_oy = after(grad_oy, *grad_x[1:])
        grad_out = mixer_finish(grad_oy[0])
        grad_out = jnp.transpose(grad_out, (0, 2, 1)).reshape(half, part).astype(F32)
        beside = lambda g: jnp.concatenate([g[0], g[1]], axis=1).astype(F32)
        grad_branch_y = beside(mixer_finish(grad_oy[1]))
        grad_x = sum(g.astype(F32) for g in grad_x).astype(BF16)
        grad_branch_x = beside(mixer_finish(grad_x))

        vec = jnp.transpose(grad_vec.reshape(8, n, slim), (1, 0, 2)).reshape(n, 1, 8 * slim)
        grad_small = jnp.concatenate(
            [
                grad_gate_a.reshape(n, gate_rows, half),
                grad_gate_in.reshape(n, gate_rows, half),
                jnp.pad(vec, ((0, 0), (0, pad_rows - 1), (0, half - 8 * slim))),
            ],
            axis=1,
        ).reshape(nz, 2, 2, 2 * gate_rows + pad_rows, half)
        grad_small = after(grad_small, grad_x_rows)
        grad_small = grid.reduce_z(grid.reduce(grid.reduce(grad_small, "x", 2), "y", 1))
        unpack = lambda g: jnp.transpose(g.reshape(gate_rows, heads, block), (1, 0, 2))
        vec = grad_small[2 * gate_rows, : 8 * slim].reshape(8, slim)

        grad_normed = contract_last(grad_in_rows, full_in).reshape(2, 2, rows_each, width)
        grad_normed = grid.reduce(grad_normed, "t", 1)
        grad_normed = grad_normed[0] + grid.swap(grad_normed[1].astype(BF16), "x").astype(F32)
        _, norm_pull = jax.vjp(scale_norm, rows, full_gain_mix)
        grad_rows, _ = norm_pull(grad_normed)
        grad_inputs = grad_resid + grad_rows

        gains = jnp.stack(
            [
                jnp.sum(
                    branch_x.astype(F32) * grad_branch_x + branch_y.astype(F32) * grad_branch_y,
                    axis=1,
                )
                / gain_mix.astype(F32),
                (sums[0] + sums[1])[:, 0]
                / gain_mlp.astype(F32),
            ]
        )
        gains = gains + grid.swap(gains, "t")
        gains = lax.dynamic_index_in_dim(gains.reshape(2, 2, split), grid.t, 1, keepdims=False)
        return (
            result,
            grad_inputs,
            gains[0],
            gains[1],
            grad_branch_x,
            grad_branch_y,
            vec[:4],
            vec[4],
            unpack(grad_small[:gate_rows]),
            vec[5],
            unpack(grad_small[gate_rows : 2 * gate_rows]),
            vec[6],
            vec[7],
            grad_out,
            grad_gate,
            grad_up,
            grad_down,
        )

    return run


def solution(mesh):
    in_specs = (
        P(("dp", "tensor"), None),
        P("dp"),
        P("dp"),
        P("dp", "tensor"),
        P("dp", "tensor"),
        P(None, ("tensor", "dp")),
        P(("tensor", "dp")),
        P("tensor", "dp", None),
        P(("tensor", "dp")),
        P("tensor", "dp", None),
        P(("tensor", "dp")),
        P(("tensor", "dp")),
        P("tensor", "dp"),
        P("dp", "tensor"),
        P("dp", "tensor"),
        P("tensor", "dp"),
        P(("dp", "tensor"), None),
    )
    out_specs = (
        P(("dp", "tensor"), None),
        P(("dp", "tensor"), None),
        P(("dp", "tensor")),
        P(("dp", "tensor")),
        P("dp", "tensor"),
        P("dp", "tensor"),
        P(None, ("tensor", "dp")),
        P(("tensor", "dp")),
        P("tensor", "dp", None),
        P(("tensor", "dp")),
        P("tensor", "dp", None),
        P(("tensor", "dp")),
        P(("tensor", "dp")),
        P("tensor", "dp"),
        P("dp", "tensor"),
        P("dp", "tensor"),
        P("tensor", "dp"),
    )
    return jax.shard_map(
        local(mesh.shape["dp"]),
        mesh=mesh,
        in_specs=in_specs,
        out_specs=out_specs,
        check_vma=False,
    )
```

```python
import math

import jax
import jax.numpy as jnp
from jax import lax
from jax.experimental import pallas as pl
from jax.experimental.pallas import tpu as pltpu
from jax.sharding import PartitionSpec as P

EPSILON = 1e-06
F32 = jnp.float32
BF16 = jnp.bfloat16


def matmul(left, right):
    return jnp.dot(left, right, preferred_element_type=F32)


def contract_last(left, right):
    return lax.dot_general(left, right, (((1,), (1,)), ((), ())), preferred_element_type=F32)


def contract_first(left, right):
    return lax.dot_general(left, right, (((0,), (0,)), ((), ())), preferred_element_type=F32)


def scale_norm(values, gain):
    return values * lax.rsqrt(jnp.mean(values * values, axis=-1, keepdims=True) + EPSILON) * gain


def down(value, by, fill):
    row = lax.broadcasted_iota(jnp.int32, value.shape, 0)
    return jnp.where(row < by, fill, pltpu.roll(value, by, 0))


def up(value, by, fill):
    length = value.shape[0]
    row = lax.broadcasted_iota(jnp.int32, value.shape, 0)
    return jnp.where(row >= length - by, fill, pltpu.roll(value, length - by, 0))


def scan(shift, decay, driven):
    by = 1
    while by < decay.shape[0]:
        driven = driven + decay * shift(driven, by, 0.0)
        if 2 * by < decay.shape[0]:
            decay = decay * shift(decay, by, 1.0)
        by *= 2
    return driven


def minus_expm1(u):
    series = 1.0 + u * (1 / 7)
    for k in (6, 5, 4, 3, 2):
        series = 1.0 + u * (1 / k) * series
    return jnp.where(u > -0.25, -u * series, 1.0 - jnp.exp(u))


def gelu_parts(v):
    inner = 0.7978845608 * (v + 0.044715 * v * v * v)
    tanh = jnp.tanh(inner)
    value = 0.5 * v * (1.0 + tanh)
    slope = 0.5 * (1.0 + tanh) + 0.5 * v * (1.0 - tanh * tanh) * 0.7978845608 * (
        1.0 + 3 * 0.044715 * v * v
    )
    return value, slope


def mixer_forward(px, py, ga, gi, vec, mixed, states, conv, rate, entry):
    taps = vec[...]
    value = px[...]
    total = taps[4:5] + taps[0:1] * value
    for k in range(1, 4):
        total = total + taps[k : k + 1] * down(value, k, 0.0)
    rounded = total.astype(BF16)
    r = jax.nn.sigmoid(matmul(rounded, ga[0]) + taps[5:6])
    e = jax.nn.sigmoid(matmul(rounded, gi[0]) + taps[6:7])
    log_decay = -8.0 * taps[7:8] * r
    driven = jnp.sqrt(minus_expm1(2.0 * log_decay)) * (e * total)
    s = scan(down, jnp.exp(log_decay), driven)
    mixed[...] = (s * gelu_parts(py[...])[0]).astype(BF16)
    states[...] = s
    conv[...] = total
    rate[...] = r
    entry[...] = e


def mixer_backward(gm, px, py, ga, gi, vec, states, conv, rate, entry, gpx, gga, ggi, gvec):
    taps = vec[...]
    s, total, r, e, grad = states[...], conv[...], rate[...], entry[...], gm[...]
    gated = gelu_parts(py[...])[0]
    log_decay = -8.0 * taps[7:8] * r
    decay = jnp.exp(log_decay)
    root = jnp.sqrt(minus_expm1(2.0 * log_decay))
    grad_driven = scan(up, up(decay, 1, 0.0), grad * gated)
    grad_decay = grad_driven * down(s, 1, 0.0)
    grad_root = grad_driven * (e * total)
    grad_log = grad_decay * decay - grad_root * (decay * decay) / root
    grad_rate = grad_log * (-8.0 * taps[7:8])
    grad_entry = grad_driven * root * total
    ra = (grad_rate * r * (1.0 - r)).astype(BF16)
    ri = (grad_entry * e * (1.0 - e)).astype(BF16)
    rounded = total.astype(BF16)
    gga[...] = contract_first(rounded, ra)
    ggi[...] = contract_first(rounded, ri)
    grad_conv = (
        grad_driven * root * e + contract_last(ra, ga[0]) + contract_last(ri, gi[0])
    )
    value = px[...]
    back = taps[0:1] * grad_conv
    sums = [jnp.sum(grad_conv * value, axis=0, keepdims=True)]
    for k in range(1, 4):
        back = back + taps[k : k + 1] * up(grad_conv, k, 0.0)
        sums.append(jnp.sum(grad_conv * down(value, k, 0.0), axis=0, keepdims=True))
    gpx[...] = back.astype(BF16)
    sums.append(jnp.sum(grad_conv, axis=0, keepdims=True))
    sums.append(jnp.sum(ra.astype(F32), axis=0, keepdims=True))
    sums.append(jnp.sum(ri.astype(F32), axis=0, keepdims=True))
    sums.append(jnp.sum(grad_log * (-8.0 * r), axis=0, keepdims=True))
    gvec[...] = jnp.concatenate(sums, axis=0)


def by_head(kernel, heads, length, block, kinds, outs):
    spec = {
        "r": pl.BlockSpec((length, block), lambda h: (0, h)),
        "g": pl.BlockSpec((1, block, block), lambda h: (h, 0, 0)),
        "v": pl.BlockSpec((8, block), lambda h: (0, h)),
        "w": pl.BlockSpec((block, block), lambda h: (0, h)),
    }
    sizes = {"r": (length, heads * block), "v": (8, heads * block), "w": (block, heads * block)}
    return pl.pallas_call(
        kernel,
        grid=(heads,),
        in_specs=[spec[k] for k in kinds],
        out_specs=[spec[k] for k, _ in outs],
        out_shape=[jax.ShapeDtypeStruct(sizes[k], d) for k, d in outs],
        compiler_params=pltpu.CompilerParams(vmem_limit_bytes=32 * 1024 * 1024),
    )


def scalar(value):
    return jnp.asarray(value, jnp.int32).reshape(1)


def whole(shape):
    return pl.BlockSpec(shape, lambda *_: (0,) * len(shape))


def params(mib):
    return pltpu.CompilerParams(vmem_limit_bytes=mib * 1024 * 1024)


def cut(values, z, nz):
    part, columns = values[0].shape
    units = columns // nz
    n = len(values)

    def kernel(where, *refs):
        for here in range(nz):

            @pl.when(where[0] == here)
            def _():
                for k in range(nz):
                    first = (here + k) % nz * units
                    for w in range(n):
                        refs[n + k][w] = refs[w][:, first : first + units]

    return pl.pallas_call(
        kernel,
        in_specs=[pl.BlockSpec(memory_space=pltpu.SMEM)] + [whole((part, columns))] * n,
        out_specs=[whole((n, part, units))] * nz,
        out_shape=[jax.ShapeDtypeStruct((n, part, units), values[0].dtype)] * nz,
        compiler_params=params(40),
    )(scalar(z), *values)


def line_up(pieces, z):
    nz = len(pieces)
    n, *rest = pieces[0].shape

    def kernel(where, *refs):
        for k in range(nz):
            to = lax.rem(where[0] - k + nz, nz)
            for w in range(n):
                refs[-1][w, to] = refs[k][w]

    return pl.pallas_call(
        kernel,
        in_specs=[pl.BlockSpec(memory_space=pltpu.SMEM)] + [whole((n, *rest))] * nz,
        out_specs=whole((n, nz, *rest)),
        out_shape=jax.ShapeDtypeStruct((n, nz, *rest), pieces[0].dtype),
        compiler_params=params(40),
    )(scalar(z), *pieces)


def norm_rows(here, across, gain, t):
    rows, width = here[0].shape

    def kernel(where, gain, *refs):
        for s in range(2):
            for other in range(2):
                value = refs[2 * s + other][...].astype(F32)
                scale = lax.rsqrt(jnp.mean(value * value, axis=-1, keepdims=True) + EPSILON)
                place = 1 - where[0] if other else where[0]
                first = pl.multiple_of((2 * s + place) * rows, rows)
                refs[4][pl.ds(first, rows), :] = (value * scale * gain[...]).astype(BF16)

    return pl.pallas_call(
        kernel,
        in_specs=[pl.BlockSpec(memory_space=pltpu.SMEM), whole((1, width))]
        + [whole((rows, width))] * 4,
        out_specs=whole((4 * rows, width)),
        out_shape=jax.ShapeDtypeStruct((4 * rows, width), BF16),
        compiler_params=params(32),
    )(scalar(t), gain.reshape(1, width), *here, *across)


def join(pieces, weights, z):
    nz = len(pieces)
    n, part, units = pieces[0].shape
    shape = weights[0].shape

    def kernel(where, *refs):
        for w in range(n):
            out, sums = refs[n + nz + w], refs[2 * n + nz + w]
            for here in range(nz):

                @pl.when(where[0] == here)
                def _():
                    for k in range(nz):
                        first = (here - k) % nz * units
                        out[:, first : first + units] = refs[n + k][w].astype(F32)

            sums[...] = jnp.sum(out[...] * refs[w][...].astype(F32), axis=1, keepdims=True)

    outs = pl.pallas_call(
        kernel,
        in_specs=[pl.BlockSpec(memory_space=pltpu.SMEM)]
        + [whole(shape)] * n
        + [whole((n, part, units))] * nz,
        out_specs=[whole(shape)] * n + [whole((part, 1))] * n,
        out_shape=[jax.ShapeDtypeStruct(shape, F32)] * n
        + [jax.ShapeDtypeStruct((part, 1), F32)] * n,
        compiler_params=params(48),
    )(scalar(z), *weights, *pieces)
    return outs[:n], outs[n:]


def reorder(value, nz, back):
    rows, width = value.shape
    part = width // (4 * nz)

    def kernel(source, out):
        for k in range(4):
            for z in range(nz):
                natural, own = (z * 4 + k) * part, (k * nz + z) * part
                to, of = (natural, own) if back else (own, natural)
                out[:, to : to + part] = source[:, of : of + part]

    return pl.pallas_call(
        kernel,
        in_specs=[whole(value.shape)],
        out_specs=whole(value.shape),
        out_shape=jax.ShapeDtypeStruct(value.shape, value.dtype),
        compiler_params=params(32),
    )(value)


TILE = 256
GATE, UP, DOWN = range(3)


def rows_of(width):
    return pl.BlockSpec((TILE, width), lambda i: (i, 0))


def weight_of(weights, which):
    corners, _, *rest = weights[0].shape
    return pl.BlockSpec((corners, 1, *rest), lambda i: (0, which % 2, 0, 0, 0))


def flat(ref):
    return ref[...].reshape(-1, ref.shape[-1])


def ffn_down_back(act, weights):
    tokens, width = act.shape
    units = weights[0].shape[-1]

    def kernel(act, down, out):
        out[...] = matmul(act[...], flat(down))

    return pl.pallas_call(
        kernel,
        grid=(tokens // TILE,),
        in_specs=[rows_of(width), weight_of(weights, DOWN)],
        out_specs=rows_of(units),
        out_shape=jax.ShapeDtypeStruct((tokens, units), F32),
        compiler_params=params(48),
    )(act, weights[1])


def ffn_middle(act, weights, grad_hidden):
    tokens, width = act.shape
    units = weights[0].shape[-1]

    def kernel(act, grad, gate, up, hidden, grads):
        value = act[...]
        gate_pre = matmul(value, flat(gate))
        up_pre = matmul(value, flat(up))
        active, slope = gelu_parts(gate_pre)
        hidden[...] = (active * up_pre).astype(BF16)
        grads[0] = (slope * (grad[...] * up_pre)).astype(BF16)
        grads[1] = (grad[...] * active).astype(BF16)

    return pl.pallas_call(
        kernel,
        grid=(tokens // TILE,),
        in_specs=[
            rows_of(width),
            rows_of(units),
            weight_of(weights, GATE),
            weight_of(weights, UP),
        ],
        out_specs=[rows_of(units), pl.BlockSpec((2, TILE, units), lambda i: (0, i, 0))],
        out_shape=[
            jax.ShapeDtypeStruct((tokens, units), BF16),
            jax.ShapeDtypeStruct((2, tokens, units), BF16),
        ],
        compiler_params=params(56),
    )(act, grad_hidden, weights[0], weights[0])


def ffn_collect(acts, weights, which, dtype):
    n, tokens, units = acts.shape
    width = math.prod(weights[1].shape[:-1])

    def kernel(acts, *refs):
        total = contract_last(acts[0], flat(refs[0]))
        for p in range(1, n):
            total = total + contract_last(acts[p], flat(refs[p]))
        refs[n][...] = total.astype(dtype)

    return pl.pallas_call(
        kernel,
        grid=(tokens // TILE,),
        in_specs=[pl.BlockSpec((n, TILE, units), lambda i: (0, i, 0))]
        + [weight_of(weights, w) for w in which],
        out_specs=rows_of(width),
        out_shape=jax.ShapeDtypeStruct((tokens, width), dtype),
        compiler_params=params(56),
    )(acts, *[weights[w // 2] for w in which])


def weight_grad(acts, grads, lead, tail, dtype, n=None, at=0, into=None):
    tokens, width = acts[0].shape
    m, _, columns = grads[0].shape
    n = n or m
    p = len(acts)
    shape = lead + tail
    block = math.prod(shape)
    at_once = math.lcm(block, 128) // block
    ones = (0,) * len(lead), (0,) * (len(tail) + 1)
    full = (width // block, *lead, n, *tail, columns)

    def kernel(*refs):
        total = contract_first(refs[0][...], refs[p][0])
        for k in range(1, p):
            total = total + contract_first(refs[k][...], refs[p + k][0])
        refs[-1][...] = total.reshape(refs[-1].shape).astype(dtype)

    return pl.pallas_call(
        kernel,
        grid=(m, width // block // at_once),
        in_specs=[pl.BlockSpec((tokens, block * at_once), lambda w, i: (0, i))] * p
        + [pl.BlockSpec((1, tokens, columns), lambda w, i: (w, 0, 0))] * p
        + ([] if into is None else [pl.BlockSpec(memory_space=pl.ANY)]),
        out_specs=pl.BlockSpec(
            (at_once, *lead, 1, *tail, columns), lambda w, i: (i, *ones[0], w + at, *ones[1])
        ),
        out_shape=jax.ShapeDtypeStruct(full, dtype),
        input_output_aliases={} if into is None else {2 * p: 0},
        compiler_params=params(48),
    )(*acts, *grads, *([] if into is None else [into]))


def after(value, *deps):
    return lax.optimization_barrier((value,) + deps)[0]


class Grid:
    def __init__(self, n):
        self.n = n
        self.nz = n // 4
        index = lax.axis_index("dp")
        self.x = index % 2
        self.y = (index // 2) % 2
        self.z = index // 4
        self.t = lax.axis_index("tensor")
        self.corners = [[4 * z + k for k in range(4)] for z in range(self.nz)]
        self.planes = [[4 * z + 2 * y + x for z in range(self.nz) for y in range(2)] for x in range(2)]

    def place(self, axis):
        return {"x": self.x, "y": self.y, "t": self.t}[axis]

    def swap(self, value, axis):
        if axis == "t":
            return lax.ppermute(value, "tensor", [(0, 1), (1, 0)])
        bit = {"x": 1, "y": 2}[axis]
        return lax.ppermute(value, "dp", [(i, i ^ bit) for i in range(self.n)])

    def shift(self, value, by):
        return lax.ppermute(value, "dp", [(i, (i + 4 * by) % self.n) for i in range(self.n)])

    def pair(self, mine, other, axis):
        here = self.place(axis)
        return jnp.where(here == 0, jnp.stack([mine, other]), jnp.stack([other, mine]))

    def pick(self, value, axis, dim, other=False):
        here = self.place(axis)
        return lax.dynamic_index_in_dim(value, 1 - here if other else here, dim, keepdims=False)

    def shifts(self, pieces):
        return [pieces[0]] + [self.shift(p, k) for k, p in enumerate(pieces) if k]

    def trade(self, value, axis):
        return self.pair(
            self.pick(value, axis, 0), self.swap(self.pick(value, axis, 0, True), axis), axis
        )

    def reduce(self, value, axis, dim):
        got = self.swap(self.pick(value, axis, dim, True).astype(BF16), axis)
        return self.pick(value, axis, dim).astype(F32) + got.astype(F32)

    def reduce_z(self, value):
        take = lambda k: lax.dynamic_index_in_dim(value, (self.z + k) % self.nz, 0, keepdims=False)
        total = take(0).astype(F32)
        for k in range(1, self.nz):
            total = total + self.shift(take(k).astype(BF16), k).astype(F32)
        return total


def local(n):
    def run(
        inputs,
        gain_mix,
        gain_mlp,
        branch_x,
        branch_y,
        conv_taps,
        conv_bias,
        gate_a,
        bias_a,
        gate_in,
        bias_in,
        decay_param,
        out_proj,
        ffn_gate,
        ffn_up,
        ffn_down,
        cotangent,
    ):
        grid = Grid(n)
        nz = grid.nz
        rows_each, width = inputs.shape
        part, half = branch_x.shape
        quarter = half // 2
        heads, gate_rows, block = gate_a.shape
        units = ffn_gate.shape[1] // nz
        split = part // 2
        run_len = nz * part
        length = 2 * rows_each
        slim = conv_bias.shape[0]
        here_x = grid.x == 0

        down_rows = jnp.transpose(ffn_down)
        slices = grid.shifts(cut((ffn_gate, ffn_up), grid.z, nz))

        vectors = jnp.concatenate(
            [conv_taps.reshape(-1), conv_bias, bias_a, bias_in, decay_param, gain_mix, gain_mlp]
        )
        pad_rows = -(2 * gate_rows + 1) % 16 + 1
        packed = jnp.concatenate(
            [
                jnp.transpose(gate_a, (1, 0, 2)).reshape(gate_rows, half),
                jnp.transpose(gate_in, (1, 0, 2)).reshape(gate_rows, half),
                jnp.pad(vectors[None], ((0, pad_rows - 1), (0, half - vectors.shape[0]))),
            ]
        )
        early = grid.shifts([after(packed[None], slices[1])] * nz)
        small = line_up(early, grid.z)[0]
        small = grid.pair(small, grid.swap(small, "y"), "y")
        small = grid.pair(small, grid.swap(small, "x"), "x")
        small = jnp.transpose(small, (2, 1, 0, 3, 4)).reshape(n, -1, half)
        gates = small[:, : 2 * gate_rows].reshape(n, 2, gate_rows, heads, block)
        gates = jnp.transpose(gates, (1, 3, 0, 2, 4)).reshape(2, heads, n * gate_rows, block)
        full_gate_a, full_gate_in = gates[0], gates[1]
        vecs = small[:, 2 * gate_rows].astype(F32)
        per = jnp.transpose(vecs[:, : 8 * slim].reshape(n, 8, slim), (1, 0, 2)).reshape(8, half)
        decay_row = per[7:8]
        per = jnp.concatenate([per[:7], jax.nn.softplus(decay_row)])
        full_gain_mix = vecs[:, 8 * slim : 8 * slim + part].reshape(width)
        full_gain_mlp = vecs[:, 8 * slim + part : 8 * slim + 2 * part].reshape(width)

        by_x = lambda w: jnp.stack([w[:, :quarter], w[:, quarter:]])
        mine = [by_x(w) for w in (branch_x, branch_y, jnp.transpose(out_proj))]
        mine = grid.trade(jnp.concatenate(mine, axis=-1), "x").reshape(2 * part, -1)
        mixer = lax.all_gather(mine, "dp", axis=0, tiled=True, axis_index_groups=grid.planes)
        full_in, full_out = mixer[:, : 2 * quarter], mixer[:, 2 * quarter :]
        across = grid.swap(after(inputs, mine), "x")

        normed = norm_rows(
            (inputs, grid.swap(inputs, "t")), (across, grid.swap(across, "t")), full_gain_mix, grid.t
        )

        def plane(own):
            return lax.all_gather(own, "dp", axis=0, tiled=True, axis_index_groups=grid.corners)

        slices = line_up(after(slices, normed, full_gate_a, full_gate_in, per), grid.z)[None]
        weights_pair = plane(after(slices, mixer))
        down_slices = grid.shifts(after(tuple(cut((down_rows,), grid.z, nz)), slices))

        def to_line(value, *deps):
            value = after(reorder(value, nz, False), *deps)
            return grid.shifts([value] * nz)

        rows = inputs.astype(F32)
        cot_line = to_line(cotangent, down_slices[1])
        pre = matmul(normed, full_in).reshape(2, length, 2 * quarter)

        def whole_half(mine, other):
            return jnp.where(
                here_x, jnp.concatenate([mine, other], 1), jnp.concatenate([other, mine], 1)
            )

        def to_rows(value):
            low, high = value[:, :quarter], value[:, quarter:]
            away = grid.swap(jnp.where(here_x, high, low), "x")
            return jnp.concatenate([jnp.where(here_x, low, high), away])

        got = grid.swap(pre[1].astype(BF16), "x").astype(F32)
        got = after(got, *down_slices[1:])
        weights_down = plane(after(line_up(down_slices, grid.z)[None], weights_pair))
        weights = (weights_pair, weights_down)
        pre_x = whole_half(pre[0, :, :quarter], got[:, :quarter])
        pre_y = whole_half(pre[0, :, quarter:], got[:, quarter:])
        mixed, states, conv, rate, entry = by_head(
            mixer_forward, heads, length, block, "rrggv", [("r", BF16)] + [("r", F32)] * 4
        )(pre_x, pre_y, full_gate_a, full_gate_in, per)
        mixed = after(to_rows(mixed), cot_line[1])
        branch_out = contract_last(mixed, full_out).reshape(2, 2, rows_each, width)
        branch_out = grid.reduce(branch_out, "t", 1)
        branch_out = branch_out[0] + grid.swap(branch_out[1].astype(BF16), "x").astype(F32)
        resid = after(rows + branch_out, *cot_line)

        normed_two_rows, norm_two_pull = jax.vjp(scale_norm, resid, full_gain_mlp)
        def from_line(acts, which, *deps):
            other = ffn_collect(acts[1], weights, which, BF16)
            other = grid.swap(other, "t")
            value = ffn_collect(acts[0], weights, which, F32) + other.astype(F32)
            value = after(value.reshape(nz, rows_each, width), *deps)
            away = [value[k].astype(BF16) for k in range(1, nz)]
            return away, [value[0]] + [grid.shift(v, -1 - k) for k, v in enumerate(away)]

        def total(got):
            return reorder(sum(g.astype(F32) for g in got), nz, True)

        def both_t(line):
            rows = jnp.concatenate(line)
            return rows, grid.swap(rows, "t")

        upstream = both_t(cot_line)
        grad_hidden = [ffn_down_back(u, weights) for u in upstream]
        normed_two = both_t(to_line(normed_two_rows.astype(BF16)))
        hidden, grad_pre = zip(
            *[ffn_middle(a, weights, g) for a, g in zip(normed_two, grad_hidden)]
        )
        hidden = [h[None] for h in hidden]
        sent, got_result = from_line(hidden, (DOWN,))
        upstream, normed_two = after((upstream, normed_two), *sent)
        grad_ffn = weight_grad(normed_two, grad_pre, (), (nz, part), BF16, 3)
        grad_ffn = weight_grad(upstream, hidden, (), (nz, part), BF16, 3, 2, grad_ffn)
        grad_pre = after(grad_pre, grad_ffn, got_result[1])
        sent, got_two = from_line(grad_pre, (GATE, UP))

        def ffn_send(value, *deps):
            value = after(value, *deps)
            take = lambda k: lax.dynamic_index_in_dim(value, (grid.z + k) % nz, 1, keepdims=False)
            return grid.shifts([take(k) for k in range(nz)])

        grad_ffn = lax.psum_scatter(
            grad_ffn, "dp", scatter_dimension=0, tiled=True, axis_index_groups=grid.corners
        )
        grad_normed_two = total(after(got_two, *got_result[1:]))
        grad_ffn = ffn_send(grad_ffn[0], got_two[1])

        grad_resid_norm, _ = norm_two_pull(grad_normed_two)
        grad_resid = cotangent.astype(F32) + grad_resid_norm
        back = grad_resid.astype(BF16)
        back = jnp.stack([back, grid.swap(back, "x")])
        back = jnp.swapaxes(grid.pair(back, grid.swap(back, "t"), "t"), 0, 1)
        back = back.reshape(2 * length, width)
        grad_mixed = matmul(back, full_out).reshape(2, length, quarter)
        grad_mixed = whole_half(
            grad_mixed[0], grid.swap(grad_mixed[1].astype(BF16), "x").astype(F32)
        )
        grad_mixed = after(grad_mixed, grad_ffn[1])
        grad_pre_y = gelu_parts(pre_y)[1] * (grad_mixed * states)
        grad_y_rows = to_rows(grad_pre_y.astype(BF16))

        def mixer_reduce(grad):
            grad = grad.reshape(nz, 2, 2, part, -1)
            away = grid.swap(grid.pick(grad, "y", 1, True).astype(BF16), "y")
            return grid.pick(grad, "y", 1), away

        def mixer_send(value, *deps):
            here, away = after(value, *deps)
            value = here + away.astype(F32)
            take = lambda k: lax.dynamic_index_in_dim(value, (grid.z + k) % nz, 0, keepdims=False)
            got = [take(0)] + [grid.shift(take(k).astype(BF16), k) for k in range(1, nz)]
            return got

        def mixer_finish(got):
            return grid.trade(got, "x")

        grad_oy = weight_grad([back], [mixed[None]], (2,), (2, part), BF16, 2)
        grad_oy = weight_grad([normed], [grad_y_rows[None]], (2,), (2, part), BF16, 2, 1, grad_oy)
        grad_oy = lax.psum_scatter(
            grad_oy.reshape(2 * nz, 2, 2, part, quarter),
            "dp",
            scatter_dimension=0,
            tiled=True,
            axis_index_groups=grid.planes,
        )[0]
        grad_pre_x, grad_gate_a, grad_gate_in, grad_vec = by_head(
            mixer_backward,
            heads,
            length,
            block,
            "rrrggvrrrr",
            [("r", BF16), ("w", F32), ("w", F32), ("v", F32)],
        )(grad_mixed, pre_x, pre_y, full_gate_a, full_gate_in, per, states, conv, rate, entry)
        grad_vec = jnp.concatenate([grad_vec[:7], grad_vec[7:] * jax.nn.sigmoid(decay_row)])
        grad_x_rows = to_rows(grad_pre_x)
        grad_x = mixer_reduce(weight_grad([normed], [grad_x_rows[None]], (), (4, part), F32))
        grad_x = mixer_send(grad_x, *grad_ffn[1:])
        grad_in_rows = jnp.concatenate([grad_x_rows, grad_y_rows], axis=1)

        result = (resid + total(got_result)).astype(BF16)
        (grad_gate, grad_up, grad_down), sums = join(
            after(grad_ffn, *grad_x[1:]), (ffn_gate, ffn_up, down_rows), grid.z
        )
        grad_down = jnp.transpose(grad_down)
        grad_oy = after(grad_oy, *grad_x[1:])
        grad_out = mixer_finish(grad_oy[0])
        grad_out = jnp.transpose(grad_out, (0, 2, 1)).reshape(half, part).astype(F32)
        beside = lambda g: jnp.concatenate([g[0], g[1]], axis=1).astype(F32)
        grad_branch_y = beside(mixer_finish(grad_oy[1]))
        grad_x = sum(g.astype(F32) for g in grad_x).astype(BF16)
        grad_branch_x = beside(mixer_finish(grad_x))

        vec = jnp.transpose(grad_vec.reshape(8, n, slim), (1, 0, 2)).reshape(n, 1, 8 * slim)
        grad_small = jnp.concatenate(
            [
                grad_gate_a.reshape(n, gate_rows, half),
                grad_gate_in.reshape(n, gate_rows, half),
                jnp.pad(vec, ((0, 0), (0, pad_rows - 1), (0, half - 8 * slim))),
            ],
            axis=1,
        ).reshape(nz, 2, 2, 2 * gate_rows + pad_rows, half)
        grad_small = after(grad_small, grad_x_rows)
        grad_small = grid.reduce_z(grid.reduce(grid.reduce(grad_small, "x", 2), "y", 1))
        unpack = lambda g: jnp.transpose(g.reshape(gate_rows, heads, block), (1, 0, 2))
        vec = grad_small[2 * gate_rows, : 8 * slim].reshape(8, slim)

        grad_normed = contract_last(grad_in_rows, full_in).reshape(2, 2, rows_each, width)
        grad_normed = grid.reduce(grad_normed, "t", 1)
        grad_normed = grad_normed[0] + grid.swap(grad_normed[1].astype(BF16), "x").astype(F32)
        _, norm_pull = jax.vjp(scale_norm, rows, full_gain_mix)
        grad_rows, _ = norm_pull(grad_normed)
        grad_inputs = grad_resid + grad_rows

        gains = jnp.stack(
            [
                jnp.sum(
                    branch_x.astype(F32) * grad_branch_x + branch_y.astype(F32) * grad_branch_y,
                    axis=1,
                )
                / gain_mix.astype(F32),
                (sums[0] + sums[1])[:, 0]
                / gain_mlp.astype(F32),
            ]
        )
        gains = gains + grid.swap(gains, "t")
        gains = lax.dynamic_index_in_dim(gains.reshape(2, 2, split), grid.t, 1, keepdims=False)
        return (
            result,
            grad_inputs,
            gains[0],
            gains[1],
            grad_branch_x,
            grad_branch_y,
            vec[:4],
            vec[4],
            unpack(grad_small[:gate_rows]),
            vec[5],
            unpack(grad_small[gate_rows : 2 * gate_rows]),
            vec[6],
            vec[7],
            grad_out,
            grad_gate,
            grad_up,
            grad_down,
        )

    return run


def solution(mesh):
    in_specs = (
        P(("dp", "tensor"), None),
        P("dp"),
        P("dp"),
        P("dp", "tensor"),
        P("dp", "tensor"),
        P(None, ("tensor", "dp")),
        P(("tensor", "dp")),
        P("tensor", "dp", None),
        P(("tensor", "dp")),
        P("tensor", "dp", None),
        P(("tensor", "dp")),
        P(("tensor", "dp")),
        P("tensor", "dp"),
        P("dp", "tensor"),
        P("dp", "tensor"),
        P("tensor", "dp"),
        P(("dp", "tensor"), None),
    )
    out_specs = (
        P(("dp", "tensor"), None),
        P(("dp", "tensor"), None),
        P(("dp", "tensor")),
        P(("dp", "tensor")),
        P("dp", "tensor"),
        P("dp", "tensor"),
        P(None, ("tensor", "dp")),
        P(("tensor", "dp")),
        P("tensor", "dp", None),
        P(("tensor", "dp")),
        P("tensor", "dp", None),
        P(("tensor", "dp")),
        P(("tensor", "dp")),
        P("tensor", "dp"),
        P("dp", "tensor"),
        P("dp", "tensor"),
        P("tensor", "dp"),
    )
    return jax.shard_map(
        local(mesh.shape["dp"]),
        mesh=mesh,
        in_specs=in_specs,
        out_specs=out_specs,
        check_vma=False,
    )
```

```python
import math

import jax
import jax.numpy as jnp
from jax import lax
from jax.experimental import pallas as pl
from jax.experimental.pallas import tpu as pltpu
from jax.sharding import PartitionSpec as P

EPSILON = 1e-06
F32 = jnp.float32
BF16 = jnp.bfloat16


def matmul(left, right):
    return jnp.dot(left, right, preferred_element_type=F32)


def contract_last(left, right):
    return lax.dot_general(left, right, (((1,), (1,)), ((), ())), preferred_element_type=F32)


def contract_first(left, right):
    return lax.dot_general(left, right, (((0,), (0,)), ((), ())), preferred_element_type=F32)


def scale_norm(values, gain):
    return values * lax.rsqrt(jnp.mean(values * values, axis=-1, keepdims=True) + EPSILON) * gain


def down(value, by, fill):
    row = lax.broadcasted_iota(jnp.int32, value.shape, 0)
    return jnp.where(row < by, fill, pltpu.roll(value, by, 0))


def up(value, by, fill):
    length = value.shape[0]
    row = lax.broadcasted_iota(jnp.int32, value.shape, 0)
    return jnp.where(row >= length - by, fill, pltpu.roll(value, length - by, 0))


def scan(shift, decay, driven):
    by = 1
    while by < decay.shape[0]:
        driven = driven + decay * shift(driven, by, 0.0)
        if 2 * by < decay.shape[0]:
            decay = decay * shift(decay, by, 1.0)
        by *= 2
    return driven


def minus_expm1(u):
    series = 1.0 + u * (1 / 7)
    for k in (6, 5, 4, 3, 2):
        series = 1.0 + u * (1 / k) * series
    return jnp.where(u > -0.25, -u * series, 1.0 - jnp.exp(u))


def gelu_parts(v):
    inner = 0.7978845608 * (v + 0.044715 * v * v * v)
    tanh = jnp.tanh(inner)
    value = 0.5 * v * (1.0 + tanh)
    slope = 0.5 * (1.0 + tanh) + 0.5 * v * (1.0 - tanh * tanh) * 0.7978845608 * (
        1.0 + 3 * 0.044715 * v * v
    )
    return value, slope


def mixer_forward(px, py, ga, gi, vec, mixed, states, conv, rate, entry):
    taps = vec[...]
    value = px[...]
    total = taps[4:5] + taps[0:1] * value
    for k in range(1, 4):
        total = total + taps[k : k + 1] * down(value, k, 0.0)
    rounded = total.astype(BF16)
    r = jax.nn.sigmoid(matmul(rounded, ga[0]) + taps[5:6])
    e = jax.nn.sigmoid(matmul(rounded, gi[0]) + taps[6:7])
    log_decay = -8.0 * taps[7:8] * r
    driven = jnp.sqrt(minus_expm1(2.0 * log_decay)) * (e * total)
    s = scan(down, jnp.exp(log_decay), driven)
    mixed[...] = (s * gelu_parts(py[...])[0]).astype(BF16)
    states[...] = s
    conv[...] = total
    rate[...] = r
    entry[...] = e


def mixer_backward(gm, px, py, ga, gi, vec, states, conv, rate, entry, gpx, gga, ggi, gvec):
    taps = vec[...]
    s, total, r, e, grad = states[...], conv[...], rate[...], entry[...], gm[...]
    gated = gelu_parts(py[...])[0]
    log_decay = -8.0 * taps[7:8] * r
    decay = jnp.exp(log_decay)
    root = jnp.sqrt(minus_expm1(2.0 * log_decay))
    grad_driven = scan(up, up(decay, 1, 0.0), grad * gated)
    grad_decay = grad_driven * down(s, 1, 0.0)
    grad_root = grad_driven * (e * total)
    grad_log = grad_decay * decay - grad_root * (decay * decay) / root
    grad_rate = grad_log * (-8.0 * taps[7:8])
    grad_entry = grad_driven * root * total
    ra = (grad_rate * r * (1.0 - r)).astype(BF16)
    ri = (grad_entry * e * (1.0 - e)).astype(BF16)
    rounded = total.astype(BF16)
    gga[...] = contract_first(rounded, ra)
    ggi[...] = contract_first(rounded, ri)
    grad_conv = (
        grad_driven * root * e + contract_last(ra, ga[0]) + contract_last(ri, gi[0])
    )
    value = px[...]
    back = taps[0:1] * grad_conv
    sums = [jnp.sum(grad_conv * value, axis=0, keepdims=True)]
    for k in range(1, 4):
        back = back + taps[k : k + 1] * up(grad_conv, k, 0.0)
        sums.append(jnp.sum(grad_conv * down(value, k, 0.0), axis=0, keepdims=True))
    gpx[...] = back.astype(BF16)
    sums.append(jnp.sum(grad_conv, axis=0, keepdims=True))
    sums.append(jnp.sum(ra.astype(F32), axis=0, keepdims=True))
    sums.append(jnp.sum(ri.astype(F32), axis=0, keepdims=True))
    sums.append(jnp.sum(grad_log * (-8.0 * r), axis=0, keepdims=True))
    gvec[...] = jnp.concatenate(sums, axis=0)


def by_head(kernel, heads, length, block, kinds, outs, flops=0):
    spec = {
        "r": pl.BlockSpec((length, block), lambda h: (0, h)),
        "g": pl.BlockSpec((1, block, block), lambda h: (h, 0, 0)),
        "v": pl.BlockSpec((8, block), lambda h: (0, h)),
        "w": pl.BlockSpec((block, block), lambda h: (0, h)),
    }
    sizes = {"r": (length, heads * block), "v": (8, heads * block), "w": (block, heads * block)}
    return pl.pallas_call(
        kernel,
        grid=(heads,),
        in_specs=[spec[k] for k in kinds],
        out_specs=[spec[k] for k, _ in outs],
        out_shape=[jax.ShapeDtypeStruct(sizes[k], d) for k, d in outs],
        cost_estimate=pl.CostEstimate(flops=flops, bytes_accessed=0, transcendentals=0),
        compiler_params=pltpu.CompilerParams(vmem_limit_bytes=32 * 1024 * 1024),
    )


def scalar(value):
    return jnp.asarray(value, jnp.int32).reshape(1)


def whole(shape):
    return pl.BlockSpec(shape, lambda *_: (0,) * len(shape))


def params(mib):
    return pltpu.CompilerParams(vmem_limit_bytes=mib * 1024 * 1024)


def cut(values, z, nz):
    part, columns = values[0].shape
    units = columns // nz
    n = len(values)

    def kernel(where, *refs):
        for here in range(nz):

            @pl.when(where[0] == here)
            def _():
                for k in range(nz):
                    first = (here + k) % nz * units
                    for w in range(n):
                        refs[n + k][w] = refs[w][:, first : first + units]

    return pl.pallas_call(
        kernel,
        in_specs=[pl.BlockSpec(memory_space=pltpu.SMEM)] + [whole((part, columns))] * n,
        out_specs=[whole((n, part, units))] * nz,
        out_shape=[jax.ShapeDtypeStruct((n, part, units), values[0].dtype)] * nz,
        compiler_params=params(40),
    )(scalar(z), *values)


def line_up(pieces, z):
    nz = len(pieces)
    n, *rest = pieces[0].shape

    def kernel(where, *refs):
        for k in range(nz):
            to = lax.rem(where[0] - k + nz, nz)
            for w in range(n):
                refs[-1][w, to] = refs[k][w]

    return pl.pallas_call(
        kernel,
        in_specs=[pl.BlockSpec(memory_space=pltpu.SMEM)] + [whole((n, *rest))] * nz,
        out_specs=whole((n, nz, *rest)),
        out_shape=jax.ShapeDtypeStruct((n, nz, *rest), pieces[0].dtype),
        compiler_params=params(40),
    )(scalar(z), *pieces)


def norm_rows(here, across, gain, t):
    rows, width = here[0].shape

    def kernel(where, gain, *refs):
        for s in range(2):
            for other in range(2):
                value = refs[2 * s + other][...].astype(F32)
                scale = lax.rsqrt(jnp.mean(value * value, axis=-1, keepdims=True) + EPSILON)
                place = 1 - where[0] if other else where[0]
                first = pl.multiple_of((2 * s + place) * rows, rows)
                refs[4][pl.ds(first, rows), :] = (value * scale * gain[...]).astype(BF16)

    return pl.pallas_call(
        kernel,
        in_specs=[pl.BlockSpec(memory_space=pltpu.SMEM), whole((1, width))]
        + [whole((rows, width))] * 4,
        out_specs=whole((4 * rows, width)),
        out_shape=jax.ShapeDtypeStruct((4 * rows, width), BF16),
        compiler_params=params(32),
    )(scalar(t), gain.reshape(1, width), *here, *across)


def join(pieces, weights, z):
    nz = len(pieces)
    n, part, units = pieces[0].shape
    shape = weights[0].shape

    def kernel(where, *refs):
        for w in range(n):
            out, sums = refs[n + nz + w], refs[2 * n + nz + w]
            for here in range(nz):

                @pl.when(where[0] == here)
                def _():
                    for k in range(nz):
                        first = (here - k) % nz * units
                        out[:, first : first + units] = refs[n + k][w].astype(F32)

            sums[...] = jnp.sum(out[...] * refs[w][...].astype(F32), axis=1, keepdims=True)

    outs = pl.pallas_call(
        kernel,
        in_specs=[pl.BlockSpec(memory_space=pltpu.SMEM)]
        + [whole(shape)] * n
        + [whole((n, part, units))] * nz,
        out_specs=[whole(shape)] * n + [whole((part, 1))] * n,
        out_shape=[jax.ShapeDtypeStruct(shape, F32)] * n
        + [jax.ShapeDtypeStruct((part, 1), F32)] * n,
        compiler_params=params(48),
    )(scalar(z), *weights, *pieces)
    return outs[:n], outs[n:]


def reorder(value, nz, back):
    rows, width = value.shape
    part = width // (4 * nz)

    def kernel(source, out):
        for k in range(4):
            for z in range(nz):
                natural, own = (z * 4 + k) * part, (k * nz + z) * part
                to, of = (natural, own) if back else (own, natural)
                out[:, to : to + part] = source[:, of : of + part]

    return pl.pallas_call(
        kernel,
        in_specs=[whole(value.shape)],
        out_specs=whole(value.shape),
        out_shape=jax.ShapeDtypeStruct(value.shape, value.dtype),
        compiler_params=params(32),
    )(value)


TILE = 256
GATE, UP, DOWN = range(3)


def rows_of(width):
    return pl.BlockSpec((TILE, width), lambda i: (i, 0))


def weight_of(weights, which):
    corners, _, *rest = weights[0].shape
    return pl.BlockSpec((corners, 1, *rest), lambda i: (0, which % 2, 0, 0, 0))


def flat(ref):
    return ref[...].reshape(-1, ref.shape[-1])


def ffn_down_back(act, weights):
    tokens, width = act.shape
    units = weights[0].shape[-1]

    def kernel(act, down, out):
        out[...] = matmul(act[...], flat(down))

    return pl.pallas_call(
        kernel,
        grid=(tokens // TILE,),
        in_specs=[rows_of(width), weight_of(weights, DOWN)],
        out_specs=rows_of(units),
        out_shape=jax.ShapeDtypeStruct((tokens, units), F32),
        compiler_params=params(48),
    )(act, weights[1])


def ffn_middle(act, weights, grad_hidden):
    tokens, width = act.shape
    units = weights[0].shape[-1]

    def kernel(act, grad, gate, up, hidden, grads):
        value = act[...]
        gate_pre = matmul(value, flat(gate))
        up_pre = matmul(value, flat(up))
        active, slope = gelu_parts(gate_pre)
        hidden[...] = (active * up_pre).astype(BF16)
        grads[0] = (slope * (grad[...] * up_pre)).astype(BF16)
        grads[1] = (grad[...] * active).astype(BF16)

    return pl.pallas_call(
        kernel,
        grid=(tokens // TILE,),
        in_specs=[
            rows_of(width),
            rows_of(units),
            weight_of(weights, GATE),
            weight_of(weights, UP),
        ],
        out_specs=[rows_of(units), pl.BlockSpec((2, TILE, units), lambda i: (0, i, 0))],
        out_shape=[
            jax.ShapeDtypeStruct((tokens, units), BF16),
            jax.ShapeDtypeStruct((2, tokens, units), BF16),
        ],
        compiler_params=params(56),
    )(act, grad_hidden, weights[0], weights[0])


def ffn_collect(acts, weights, which, dtype):
    n, tokens, units = acts.shape
    width = math.prod(weights[1].shape[:-1])

    def kernel(acts, *refs):
        total = contract_last(acts[0], flat(refs[0]))
        for p in range(1, n):
            total = total + contract_last(acts[p], flat(refs[p]))
        refs[n][...] = total.astype(dtype)

    return pl.pallas_call(
        kernel,
        grid=(tokens // TILE,),
        in_specs=[pl.BlockSpec((n, TILE, units), lambda i: (0, i, 0))]
        + [weight_of(weights, w) for w in which],
        out_specs=rows_of(width),
        out_shape=jax.ShapeDtypeStruct((tokens, width), dtype),
        compiler_params=params(56),
    )(acts, *[weights[w // 2] for w in which])


def weight_grad(acts, grads, lead, tail, dtype, n=None, at=0, into=None):
    tokens, width = acts[0].shape
    m, _, columns = grads[0].shape
    n = n or m
    p = len(acts)
    shape = lead + tail
    block = math.prod(shape)
    at_once = math.lcm(block, 128) // block
    ones = (0,) * len(lead), (0,) * (len(tail) + 1)
    full = (width // block, *lead, n, *tail, columns)

    def kernel(*refs):
        total = contract_first(refs[0][...], refs[p][0])
        for k in range(1, p):
            total = total + contract_first(refs[k][...], refs[p + k][0])
        refs[-1][...] = total.reshape(refs[-1].shape).astype(dtype)

    return pl.pallas_call(
        kernel,
        grid=(m, width // block // at_once),
        in_specs=[pl.BlockSpec((tokens, block * at_once), lambda w, i: (0, i))] * p
        + [pl.BlockSpec((1, tokens, columns), lambda w, i: (w, 0, 0))] * p
        + ([] if into is None else [pl.BlockSpec(memory_space=pl.ANY)]),
        out_specs=pl.BlockSpec(
            (at_once, *lead, 1, *tail, columns), lambda w, i: (i, *ones[0], w + at, *ones[1])
        ),
        out_shape=jax.ShapeDtypeStruct(full, dtype),
        input_output_aliases={} if into is None else {2 * p: 0},
        cost_estimate=pl.CostEstimate(flops=20000000000, bytes_accessed=0, transcendentals=0),
        compiler_params=params(48),
    )(*acts, *grads, *([] if into is None else [into]))


def after(value, *deps):
    return lax.optimization_barrier((value,) + deps)[0]


class Grid:
    def __init__(self, n):
        self.n = n
        self.nz = n // 4
        index = lax.axis_index("dp")
        self.x = index % 2
        self.y = (index // 2) % 2
        self.z = index // 4
        self.t = lax.axis_index("tensor")
        self.corners = [[4 * z + k for k in range(4)] for z in range(self.nz)]
        self.planes = [[4 * z + 2 * y + x for z in range(self.nz) for y in range(2)] for x in range(2)]

    def place(self, axis):
        return {"x": self.x, "y": self.y, "t": self.t}[axis]

    def swap(self, value, axis):
        if axis == "t":
            return lax.ppermute(value, "tensor", [(0, 1), (1, 0)])
        bit = {"x": 1, "y": 2}[axis]
        return lax.ppermute(value, "dp", [(i, i ^ bit) for i in range(self.n)])

    def shift(self, value, by):
        return lax.ppermute(value, "dp", [(i, (i + 4 * by) % self.n) for i in range(self.n)])

    def pair(self, mine, other, axis):
        here = self.place(axis)
        return jnp.where(here == 0, jnp.stack([mine, other]), jnp.stack([other, mine]))

    def pick(self, value, axis, dim, other=False):
        here = self.place(axis)
        return lax.dynamic_index_in_dim(value, 1 - here if other else here, dim, keepdims=False)

    def shifts(self, pieces):
        return [pieces[0]] + [self.shift(p, k) for k, p in enumerate(pieces) if k]

    def trade(self, value, axis):
        return self.pair(
            self.pick(value, axis, 0), self.swap(self.pick(value, axis, 0, True), axis), axis
        )

    def reduce(self, value, axis, dim):
        got = self.swap(self.pick(value, axis, dim, True).astype(BF16), axis)
        return self.pick(value, axis, dim).astype(F32) + got.astype(F32)

    def reduce_z(self, value):
        take = lambda k: lax.dynamic_index_in_dim(value, (self.z + k) % self.nz, 0, keepdims=False)
        total = take(0).astype(F32)
        for k in range(1, self.nz):
            total = total + self.shift(take(k).astype(BF16), k).astype(F32)
        return total


def local(n):
    def run(
        inputs,
        gain_mix,
        gain_mlp,
        branch_x,
        branch_y,
        conv_taps,
        conv_bias,
        gate_a,
        bias_a,
        gate_in,
        bias_in,
        decay_param,
        out_proj,
        ffn_gate,
        ffn_up,
        ffn_down,
        cotangent,
    ):
        grid = Grid(n)
        nz = grid.nz
        rows_each, width = inputs.shape
        part, half = branch_x.shape
        quarter = half // 2
        heads, gate_rows, block = gate_a.shape
        units = ffn_gate.shape[1] // nz
        split = part // 2
        run_len = nz * part
        length = 2 * rows_each
        slim = conv_bias.shape[0]
        here_x = grid.x == 0

        down_rows = jnp.transpose(ffn_down)
        slices = grid.shifts(cut((ffn_gate, ffn_up), grid.z, nz))

        vectors = jnp.concatenate(
            [conv_taps.reshape(-1), conv_bias, bias_a, bias_in, decay_param, gain_mix, gain_mlp]
        )
        pad_rows = -(2 * gate_rows + 1) % 16 + 1
        packed = jnp.concatenate(
            [
                jnp.transpose(gate_a, (1, 0, 2)).reshape(gate_rows, half),
                jnp.transpose(gate_in, (1, 0, 2)).reshape(gate_rows, half),
                jnp.pad(vectors[None], ((0, pad_rows - 1), (0, half - vectors.shape[0]))),
            ]
        )
        early = grid.shifts([after(packed[None], slices[1])] * nz)
        small = line_up(early, grid.z)[0]
        small = grid.pair(small, grid.swap(small, "y"), "y")
        small = grid.pair(small, grid.swap(small, "x"), "x")
        small = jnp.transpose(small, (2, 1, 0, 3, 4)).reshape(n, -1, half)
        gates = small[:, : 2 * gate_rows].reshape(n, 2, gate_rows, heads, block)
        gates = jnp.transpose(gates, (1, 3, 0, 2, 4)).reshape(2, heads, n * gate_rows, block)
        full_gate_a, full_gate_in = gates[0], gates[1]
        vecs = small[:, 2 * gate_rows].astype(F32)
        per = jnp.transpose(vecs[:, : 8 * slim].reshape(n, 8, slim), (1, 0, 2)).reshape(8, half)
        decay_row = per[7:8]
        per = jnp.concatenate([per[:7], jax.nn.softplus(decay_row)])
        full_gain_mix = vecs[:, 8 * slim : 8 * slim + part].reshape(width)
        full_gain_mlp = vecs[:, 8 * slim + part : 8 * slim + 2 * part].reshape(width)

        by_x = lambda w: jnp.stack([w[:, :quarter], w[:, quarter:]])
        mine = [by_x(w) for w in (branch_x, branch_y, jnp.transpose(out_proj))]
        mine = grid.trade(jnp.concatenate(mine, axis=-1), "x").reshape(2 * part, -1)
        mixer = lax.all_gather(mine, "dp", axis=0, tiled=True, axis_index_groups=grid.planes)
        full_in, full_out = mixer[:, : 2 * quarter], mixer[:, 2 * quarter :]
        across = grid.swap(after(inputs, mine), "x")

        normed = norm_rows(
            (inputs, grid.swap(inputs, "t")), (across, grid.swap(across, "t")), full_gain_mix, grid.t
        )

        def plane(own):
            return lax.all_gather(own, "dp", axis=0, tiled=True, axis_index_groups=grid.corners)

        slices = line_up(after(slices, normed, full_gate_a, full_gate_in, per), grid.z)[None]
        weights_pair = plane(after(slices, mixer))
        down_slices = grid.shifts(after(tuple(cut((down_rows,), grid.z, nz)), slices))

        def to_line(value, *deps):
            value = after(reorder(value, nz, False), *deps)
            return grid.shifts([value] * nz)

        rows = inputs.astype(F32)
        cot_line = to_line(cotangent, down_slices[1])
        pre = matmul(normed, full_in).reshape(2, length, 2 * quarter)

        def whole_half(mine, other):
            return jnp.where(
                here_x, jnp.concatenate([mine, other], 1), jnp.concatenate([other, mine], 1)
            )

        def to_rows(value):
            low, high = value[:, :quarter], value[:, quarter:]
            away = grid.swap(jnp.where(here_x, high, low), "x")
            return jnp.concatenate([jnp.where(here_x, low, high), away])

        got = grid.swap(pre[1].astype(BF16), "x").astype(F32)
        got = after(got, *down_slices[1:])
        weights_down = plane(after(line_up(down_slices, grid.z)[None], weights_pair))
        weights = (weights_pair, weights_down)
        pre_x = whole_half(pre[0, :, :quarter], got[:, :quarter])
        pre_y = whole_half(pre[0, :, quarter:], got[:, quarter:])
        mixed, states, conv, rate, entry = by_head(
            mixer_forward, heads, length, block, "rrggv", [("r", BF16)] + [("r", F32)] * 4, 30000000000
        )(pre_x, pre_y, full_gate_a, full_gate_in, per)
        mixed = after(to_rows(mixed), cot_line[1])
        branch_out = contract_last(mixed, full_out).reshape(2, 2, rows_each, width)
        branch_out = grid.reduce(branch_out, "t", 1)
        branch_out = branch_out[0] + grid.swap(branch_out[1].astype(BF16), "x").astype(F32)
        resid = after(rows + branch_out, *cot_line)

        normed_two_rows, norm_two_pull = jax.vjp(scale_norm, resid, full_gain_mlp)
        def from_line(acts, which, *deps):
            other = ffn_collect(acts[1], weights, which, BF16)
            other = grid.swap(other, "t")
            value = ffn_collect(acts[0], weights, which, F32) + other.astype(F32)
            value = after(value.reshape(nz, rows_each, width), *deps)
            away = [value[k].astype(BF16) for k in range(1, nz)]
            return away, [value[0]] + [grid.shift(v, -1 - k) for k, v in enumerate(away)]

        def total(got):
            return reorder(sum(g.astype(F32) for g in got), nz, True)

        def both_t(line):
            rows = jnp.concatenate(line)
            return rows, grid.swap(rows, "t")

        upstream = both_t(cot_line)
        grad_hidden = [ffn_down_back(u, weights) for u in upstream]
        normed_two = both_t(to_line(normed_two_rows.astype(BF16)))
        hidden, grad_pre = zip(
            *[ffn_middle(a, weights, g) for a, g in zip(normed_two, grad_hidden)]
        )
        hidden = [h[None] for h in hidden]
        sent, got_result = from_line(hidden, (DOWN,))
        upstream, normed_two = after((upstream, normed_two), *sent)
        grad_ffn = weight_grad(normed_two, grad_pre, (), (nz, part), BF16, 3)
        grad_ffn = weight_grad(upstream, hidden, (), (nz, part), BF16, 3, 2, grad_ffn)
        grad_pre = after(grad_pre, grad_ffn, got_result[1])
        sent, got_two = from_line(grad_pre, (GATE, UP))

        def ffn_send(value, *deps):
            value = after(value, *deps)
            take = lambda k: lax.dynamic_index_in_dim(value, (grid.z + k) % nz, 1, keepdims=False)
            return grid.shifts([take(k) for k in range(nz)])

        grad_ffn = lax.psum_scatter(
            after(grad_ffn, got_result[1]), "dp", scatter_dimension=0, tiled=True, axis_index_groups=grid.corners
        )
        grad_normed_two = total(after(got_two, *got_result[1:]))
        grad_ffn = ffn_send(grad_ffn[0], got_two[1])

        grad_resid_norm, _ = norm_two_pull(grad_normed_two)
        grad_resid = cotangent.astype(F32) + grad_resid_norm
        back = grad_resid.astype(BF16)
        back = jnp.stack([back, grid.swap(back, "x")])
        back = jnp.swapaxes(grid.pair(back, grid.swap(back, "t"), "t"), 0, 1)
        back = back.reshape(2 * length, width)
        grad_mixed = matmul(back, full_out).reshape(2, length, quarter)
        grad_mixed = whole_half(
            grad_mixed[0], grid.swap(grad_mixed[1].astype(BF16), "x").astype(F32)
        )
        grad_mixed = after(grad_mixed, grad_ffn[1])
        grad_pre_y = gelu_parts(pre_y)[1] * (grad_mixed * states)
        grad_y_rows = to_rows(grad_pre_y.astype(BF16))

        def mixer_reduce(grad):
            grad = grad.reshape(nz, 2, 2, part, -1)
            away = grid.swap(grid.pick(grad, "y", 1, True).astype(BF16), "y")
            return grid.pick(grad, "y", 1), away

        def mixer_send(value, *deps):
            here, away = after(value, *deps)
            value = here + away.astype(F32)
            take = lambda k: lax.dynamic_index_in_dim(value, (grid.z + k) % nz, 0, keepdims=False)
            got = [take(0)] + [grid.shift(take(k).astype(BF16), k) for k in range(1, nz)]
            return got

        def mixer_finish(got):
            return grid.trade(got, "x")

        grad_oy = weight_grad([back], [mixed[None]], (2,), (2, part), BF16, 2)
        grad_oy = weight_grad([normed], [grad_y_rows[None]], (2,), (2, part), BF16, 2, 1, grad_oy)
        grad_oy = lax.psum_scatter(
            grad_oy.reshape(2 * nz, 2, 2, part, quarter),
            "dp",
            scatter_dimension=0,
            tiled=True,
            axis_index_groups=grid.planes,
        )[0]
        grad_pre_x, grad_gate_a, grad_gate_in, grad_vec = by_head(
            mixer_backward,
            heads,
            length,
            block,
            "rrrggvrrrr",
            [("r", BF16), ("w", F32), ("w", F32), ("v", F32)],
            30000000000,
        )(grad_mixed, pre_x, pre_y, full_gate_a, full_gate_in, per, states, conv, rate, entry)
        grad_vec = jnp.concatenate([grad_vec[:7], grad_vec[7:] * jax.nn.sigmoid(decay_row)])
        grad_x_rows = to_rows(grad_pre_x)
        grad_x = mixer_reduce(weight_grad([normed], [grad_x_rows[None]], (), (4, part), F32))
        grad_x = mixer_send(grad_x, *grad_ffn[1:])
        grad_in_rows = jnp.concatenate([grad_x_rows, grad_y_rows], axis=1)

        result = (resid + total(got_result)).astype(BF16)
        (grad_gate, grad_up, grad_down), sums = join(
            after(grad_ffn, *grad_x[1:]), (ffn_gate, ffn_up, down_rows), grid.z
        )
        grad_down = jnp.transpose(grad_down)
        grad_oy = after(grad_oy, *grad_x[1:])
        grad_out = mixer_finish(grad_oy[0])
        grad_out = jnp.transpose(grad_out, (0, 2, 1)).reshape(half, part).astype(F32)
        beside = lambda g: jnp.concatenate([g[0], g[1]], axis=1).astype(F32)
        grad_branch_y = beside(mixer_finish(grad_oy[1]))
        grad_x = sum(g.astype(F32) for g in grad_x).astype(BF16)
        grad_branch_x = beside(mixer_finish(grad_x))

        vec = jnp.transpose(grad_vec.reshape(8, n, slim), (1, 0, 2)).reshape(n, 1, 8 * slim)
        grad_small = jnp.concatenate(
            [
                grad_gate_a.reshape(n, gate_rows, half),
                grad_gate_in.reshape(n, gate_rows, half),
                jnp.pad(vec, ((0, 0), (0, pad_rows - 1), (0, half - 8 * slim))),
            ],
            axis=1,
        ).reshape(nz, 2, 2, 2 * gate_rows + pad_rows, half)
        grad_small = after(grad_small, grad_x_rows)
        grad_small = grid.reduce_z(grid.reduce(grid.reduce(grad_small, "x", 2), "y", 1))
        unpack = lambda g: jnp.transpose(g.reshape(gate_rows, heads, block), (1, 0, 2))
        vec = grad_small[2 * gate_rows, : 8 * slim].reshape(8, slim)

        grad_normed = contract_last(grad_in_rows, full_in).reshape(2, 2, rows_each, width)
        grad_normed = grid.reduce(grad_normed, "t", 1)
        grad_normed = grad_normed[0] + grid.swap(grad_normed[1].astype(BF16), "x").astype(F32)
        _, norm_pull = jax.vjp(scale_norm, rows, full_gain_mix)
        grad_rows, _ = norm_pull(grad_normed)
        grad_inputs = grad_resid + grad_rows

        gains = jnp.stack(
            [
                jnp.sum(
                    branch_x.astype(F32) * grad_branch_x + branch_y.astype(F32) * grad_branch_y,
                    axis=1,
                )
                / gain_mix.astype(F32),
                (sums[0] + sums[1])[:, 0]
                / gain_mlp.astype(F32),
            ]
        )
        gains = gains + grid.swap(gains, "t")
        gains = lax.dynamic_index_in_dim(gains.reshape(2, 2, split), grid.t, 1, keepdims=False)
        return (
            result,
            grad_inputs,
            gains[0],
            gains[1],
            grad_branch_x,
            grad_branch_y,
            vec[:4],
            vec[4],
            unpack(grad_small[:gate_rows]),
            vec[5],
            unpack(grad_small[gate_rows : 2 * gate_rows]),
            vec[6],
            vec[7],
            grad_out,
            grad_gate,
            grad_up,
            grad_down,
        )

    return run


def solution(mesh):
    in_specs = (
        P(("dp", "tensor"), None),
        P("dp"),
        P("dp"),
        P("dp", "tensor"),
        P("dp", "tensor"),
        P(None, ("tensor", "dp")),
        P(("tensor", "dp")),
        P("tensor", "dp", None),
        P(("tensor", "dp")),
        P("tensor", "dp", None),
        P(("tensor", "dp")),
        P(("tensor", "dp")),
        P("tensor", "dp"),
        P("dp", "tensor"),
        P("dp", "tensor"),
        P("tensor", "dp"),
        P(("dp", "tensor"), None),
    )
    out_specs = (
        P(("dp", "tensor"), None),
        P(("dp", "tensor"), None),
        P(("dp", "tensor")),
        P(("dp", "tensor")),
        P("dp", "tensor"),
        P("dp", "tensor"),
        P(None, ("tensor", "dp")),
        P(("tensor", "dp")),
        P("tensor", "dp", None),
        P(("tensor", "dp")),
        P("tensor", "dp", None),
        P(("tensor", "dp")),
        P(("tensor", "dp")),
        P("tensor", "dp"),
        P("dp", "tensor"),
        P("dp", "tensor"),
        P("tensor", "dp"),
    )
    return jax.shard_map(
        local(mesh.shape["dp"]),
        mesh=mesh,
        in_specs=in_specs,
        out_specs=out_specs,
        check_vma=False,
    )
```

```python
import math

import jax
import jax.numpy as jnp
from jax import lax
from jax.experimental import pallas as pl
from jax.experimental.pallas import tpu as pltpu
from jax.sharding import PartitionSpec as P

EPSILON = 1e-06
F32 = jnp.float32
BF16 = jnp.bfloat16


def matmul(left, right):
    return jnp.dot(left, right, preferred_element_type=F32)


def contract_last(left, right):
    return lax.dot_general(left, right, (((1,), (1,)), ((), ())), preferred_element_type=F32)


def contract_first(left, right):
    return lax.dot_general(left, right, (((0,), (0,)), ((), ())), preferred_element_type=F32)


def scale_norm(values, gain):
    return values * lax.rsqrt(jnp.mean(values * values, axis=-1, keepdims=True) + EPSILON) * gain


def down(value, by, fill):
    row = lax.broadcasted_iota(jnp.int32, value.shape, 0)
    return jnp.where(row < by, fill, pltpu.roll(value, by, 0))


def up(value, by, fill):
    length = value.shape[0]
    row = lax.broadcasted_iota(jnp.int32, value.shape, 0)
    return jnp.where(row >= length - by, fill, pltpu.roll(value, length - by, 0))


def scan(shift, decay, driven):
    by = 1
    while by < decay.shape[0]:
        driven = driven + decay * shift(driven, by, 0.0)
        if 2 * by < decay.shape[0]:
            decay = decay * shift(decay, by, 1.0)
        by *= 2
    return driven


def minus_expm1(u):
    series = 1.0 + u * (1 / 7)
    for k in (6, 5, 4, 3, 2):
        series = 1.0 + u * (1 / k) * series
    return jnp.where(u > -0.25, -u * series, 1.0 - jnp.exp(u))


def gelu_parts(v):
    inner = 0.7978845608 * (v + 0.044715 * v * v * v)
    tanh = jnp.tanh(inner)
    value = 0.5 * v * (1.0 + tanh)
    slope = 0.5 * (1.0 + tanh) + 0.5 * v * (1.0 - tanh * tanh) * 0.7978845608 * (
        1.0 + 3 * 0.044715 * v * v
    )
    return value, slope


def mixer_forward(px, py, ga, gi, vec, mixed, states, conv, rate, entry):
    taps = vec[...]
    value = px[...]
    total = taps[4:5] + taps[0:1] * value
    for k in range(1, 4):
        total = total + taps[k : k + 1] * down(value, k, 0.0)
    rounded = total.astype(BF16)
    r = jax.nn.sigmoid(matmul(rounded, ga[0]) + taps[5:6])
    e = jax.nn.sigmoid(matmul(rounded, gi[0]) + taps[6:7])
    log_decay = -8.0 * taps[7:8] * r
    driven = jnp.sqrt(minus_expm1(2.0 * log_decay)) * (e * total)
    s = scan(down, jnp.exp(log_decay), driven)
    mixed[...] = (s * gelu_parts(py[...])[0]).astype(BF16)
    states[...] = s
    conv[...] = total
    rate[...] = r
    entry[...] = e


def mixer_backward(gm, px, py, ga, gi, vec, states, conv, rate, entry, gpx, gga, ggi, gvec):
    taps = vec[...]
    s, total, r, e, grad = states[...], conv[...], rate[...], entry[...], gm[...]
    gated = gelu_parts(py[...])[0]
    log_decay = -8.0 * taps[7:8] * r
    decay = jnp.exp(log_decay)
    root = jnp.sqrt(minus_expm1(2.0 * log_decay))
    grad_driven = scan(up, up(decay, 1, 0.0), grad * gated)
    grad_decay = grad_driven * down(s, 1, 0.0)
    grad_root = grad_driven * (e * total)
    grad_log = grad_decay * decay - grad_root * (decay * decay) / root
    grad_rate = grad_log * (-8.0 * taps[7:8])
    grad_entry = grad_driven * root * total
    ra = (grad_rate * r * (1.0 - r)).astype(BF16)
    ri = (grad_entry * e * (1.0 - e)).astype(BF16)
    rounded = total.astype(BF16)
    gga[...] = contract_first(rounded, ra)
    ggi[...] = contract_first(rounded, ri)
    grad_conv = (
        grad_driven * root * e + contract_last(ra, ga[0]) + contract_last(ri, gi[0])
    )
    value = px[...]
    back = taps[0:1] * grad_conv
    sums = [jnp.sum(grad_conv * value, axis=0, keepdims=True)]
    for k in range(1, 4):
        back = back + taps[k : k + 1] * up(grad_conv, k, 0.0)
        sums.append(jnp.sum(grad_conv * down(value, k, 0.0), axis=0, keepdims=True))
    gpx[...] = back.astype(BF16)
    sums.append(jnp.sum(grad_conv, axis=0, keepdims=True))
    sums.append(jnp.sum(ra.astype(F32), axis=0, keepdims=True))
    sums.append(jnp.sum(ri.astype(F32), axis=0, keepdims=True))
    sums.append(jnp.sum(grad_log * (-8.0 * r), axis=0, keepdims=True))
    gvec[...] = jnp.concatenate(sums, axis=0)


def by_head(kernel, heads, length, block, kinds, outs, flops=0):
    spec = {
        "r": pl.BlockSpec((length, block), lambda h: (0, h)),
        "g": pl.BlockSpec((1, block, block), lambda h: (h, 0, 0)),
        "v": pl.BlockSpec((8, block), lambda h: (0, h)),
        "w": pl.BlockSpec((block, block), lambda h: (0, h)),
    }
    sizes = {"r": (length, heads * block), "v": (8, heads * block), "w": (block, heads * block)}
    return pl.pallas_call(
        kernel,
        grid=(heads,),
        in_specs=[spec[k] for k in kinds],
        out_specs=[spec[k] for k, _ in outs],
        out_shape=[jax.ShapeDtypeStruct(sizes[k], d) for k, d in outs],
        cost_estimate=pl.CostEstimate(flops=flops, bytes_accessed=0, transcendentals=0),
        compiler_params=pltpu.CompilerParams(vmem_limit_bytes=32 * 1024 * 1024),
    )


def scalar(value):
    return jnp.asarray(value, jnp.int32).reshape(1)


def whole(shape):
    return pl.BlockSpec(shape, lambda *_: (0,) * len(shape))


def params(mib):
    return pltpu.CompilerParams(vmem_limit_bytes=mib * 1024 * 1024)


def cut(values, z, nz):
    part, columns = values[0].shape
    units = columns // nz
    n = len(values)

    def kernel(where, *refs):
        for here in range(nz):

            @pl.when(where[0] == here)
            def _():
                for k in range(nz):
                    first = (here + k) % nz * units
                    for w in range(n):
                        refs[n + k][w] = refs[w][:, first : first + units]

    return pl.pallas_call(
        kernel,
        in_specs=[pl.BlockSpec(memory_space=pltpu.SMEM)] + [whole((part, columns))] * n,
        out_specs=[whole((n, part, units))] * nz,
        out_shape=[jax.ShapeDtypeStruct((n, part, units), values[0].dtype)] * nz,
        compiler_params=params(40),
    )(scalar(z), *values)


def line_up(pieces, z):
    nz = len(pieces)
    n, *rest = pieces[0].shape

    def kernel(where, *refs):
        for k in range(nz):
            to = lax.rem(where[0] - k + nz, nz)
            for w in range(n):
                refs[-1][w, to] = refs[k][w]

    return pl.pallas_call(
        kernel,
        in_specs=[pl.BlockSpec(memory_space=pltpu.SMEM)] + [whole((n, *rest))] * nz,
        out_specs=whole((n, nz, *rest)),
        out_shape=jax.ShapeDtypeStruct((n, nz, *rest), pieces[0].dtype),
        compiler_params=params(40),
    )(scalar(z), *pieces)


def norm_rows(here, across, gain, t):
    rows, width = here[0].shape

    def kernel(where, gain, *refs):
        for s in range(2):
            for other in range(2):
                value = refs[2 * s + other][...].astype(F32)
                scale = lax.rsqrt(jnp.mean(value * value, axis=-1, keepdims=True) + EPSILON)
                place = 1 - where[0] if other else where[0]
                first = pl.multiple_of((2 * s + place) * rows, rows)
                refs[4][pl.ds(first, rows), :] = (value * scale * gain[...]).astype(BF16)

    return pl.pallas_call(
        kernel,
        in_specs=[pl.BlockSpec(memory_space=pltpu.SMEM), whole((1, width))]
        + [whole((rows, width))] * 4,
        out_specs=whole((4 * rows, width)),
        out_shape=jax.ShapeDtypeStruct((4 * rows, width), BF16),
        compiler_params=params(32),
    )(scalar(t), gain.reshape(1, width), *here, *across)


def join(pieces, weights, z):
    nz = len(pieces)
    n, part, units = pieces[0].shape
    shape = weights[0].shape

    def kernel(where, *refs):
        for w in range(n):
            out, sums = refs[n + nz + w], refs[2 * n + nz + w]
            for here in range(nz):

                @pl.when(where[0] == here)
                def _():
                    for k in range(nz):
                        first = (here - k) % nz * units
                        out[:, first : first + units] = refs[n + k][w].astype(F32)

            sums[...] = jnp.sum(out[...] * refs[w][...].astype(F32), axis=1, keepdims=True)

    outs = pl.pallas_call(
        kernel,
        in_specs=[pl.BlockSpec(memory_space=pltpu.SMEM)]
        + [whole(shape)] * n
        + [whole((n, part, units))] * nz,
        out_specs=[whole(shape)] * n + [whole((part, 1))] * n,
        out_shape=[jax.ShapeDtypeStruct(shape, F32)] * n
        + [jax.ShapeDtypeStruct((part, 1), F32)] * n,
        compiler_params=params(48),
    )(scalar(z), *weights, *pieces)
    return outs[:n], outs[n:]


def reorder(value, nz, back):
    rows, width = value.shape
    part = width // (4 * nz)

    def kernel(source, out):
        for k in range(4):
            for z in range(nz):
                natural, own = (z * 4 + k) * part, (k * nz + z) * part
                to, of = (natural, own) if back else (own, natural)
                out[:, to : to + part] = source[:, of : of + part]

    return pl.pallas_call(
        kernel,
        in_specs=[whole(value.shape)],
        out_specs=whole(value.shape),
        out_shape=jax.ShapeDtypeStruct(value.shape, value.dtype),
        compiler_params=params(32),
    )(value)


TILE = 256
GATE, UP, DOWN = range(3)


def rows_of(width):
    return pl.BlockSpec((TILE, width), lambda i: (i, 0))


def weight_of(weights, which):
    corners, _, *rest = weights[0].shape
    return pl.BlockSpec((corners, 1, *rest), lambda i: (0, which % 2, 0, 0, 0))


def flat(ref):
    return ref[...].reshape(-1, ref.shape[-1])


def ffn_middle(act, weights, upstream):
    tokens, width = act.shape
    units = weights[0].shape[-1]

    def kernel(act, upstream, gate, up, down, hidden, grads):
        value = act[...]
        grad = matmul(upstream[...], flat(down))
        gate_pre = matmul(value, flat(gate))
        up_pre = matmul(value, flat(up))
        active, slope = gelu_parts(gate_pre)
        hidden[...] = (active * up_pre).astype(BF16)
        grads[0] = (slope * (grad * up_pre)).astype(BF16)
        grads[1] = (grad * active).astype(BF16)

    return pl.pallas_call(
        kernel,
        grid=(tokens // TILE,),
        in_specs=[
            rows_of(width),
            rows_of(width),
            weight_of(weights, GATE),
            weight_of(weights, UP),
            weight_of(weights, DOWN),
        ],
        out_specs=[rows_of(units), pl.BlockSpec((2, TILE, units), lambda i: (0, i, 0))],
        out_shape=[
            jax.ShapeDtypeStruct((tokens, units), BF16),
            jax.ShapeDtypeStruct((2, tokens, units), BF16),
        ],
        compiler_params=params(56),
    )(act, upstream, weights[0], weights[0], weights[1])


def ffn_collect(acts, weights, which, dtype):
    n, tokens, units = acts.shape
    width = math.prod(weights[1].shape[:-1])

    def kernel(acts, *refs):
        total = contract_last(acts[0], flat(refs[0]))
        for p in range(1, n):
            total = total + contract_last(acts[p], flat(refs[p]))
        refs[n][...] = total.astype(dtype)

    return pl.pallas_call(
        kernel,
        grid=(tokens // TILE,),
        in_specs=[pl.BlockSpec((n, TILE, units), lambda i: (0, i, 0))]
        + [weight_of(weights, w) for w in which],
        out_specs=rows_of(width),
        out_shape=jax.ShapeDtypeStruct((tokens, width), dtype),
        compiler_params=params(56),
    )(acts, *[weights[w // 2] for w in which])


def weight_grad(acts, grads, lead, tail, dtype, n=None, at=0, into=None):
    tokens, width = acts[0].shape
    m, _, columns = grads[0].shape
    n = n or m
    p = len(acts)
    shape = lead + tail
    block = math.prod(shape)
    at_once = math.lcm(block, 128) // block
    ones = (0,) * len(lead), (0,) * (len(tail) + 1)
    full = (width // block, *lead, n, *tail, columns)

    def kernel(*refs):
        total = contract_first(refs[0][...], refs[p][0])
        for k in range(1, p):
            total = total + contract_first(refs[k][...], refs[p + k][0])
        refs[-1][...] = total.reshape(refs[-1].shape).astype(dtype)

    return pl.pallas_call(
        kernel,
        grid=(m, width // block // at_once),
        in_specs=[pl.BlockSpec((tokens, block * at_once), lambda w, i: (0, i))] * p
        + [pl.BlockSpec((1, tokens, columns), lambda w, i: (w, 0, 0))] * p
        + ([] if into is None else [pl.BlockSpec(memory_space=pl.ANY)]),
        out_specs=pl.BlockSpec(
            (at_once, *lead, 1, *tail, columns), lambda w, i: (i, *ones[0], w + at, *ones[1])
        ),
        out_shape=jax.ShapeDtypeStruct(full, dtype),
        input_output_aliases={} if into is None else {2 * p: 0},
        cost_estimate=pl.CostEstimate(flops=20000000000, bytes_accessed=0, transcendentals=0),
        compiler_params=params(48),
    )(*acts, *grads, *([] if into is None else [into]))


def after(value, *deps):
    return lax.optimization_barrier((value,) + deps)[0]


class Grid:
    def __init__(self, n):
        self.n = n
        self.nz = n // 4
        index = lax.axis_index("dp")
        self.x = index % 2
        self.y = (index // 2) % 2
        self.z = index // 4
        self.t = lax.axis_index("tensor")
        self.corners = [[4 * z + k for k in range(4)] for z in range(self.nz)]
        self.planes = [[4 * z + 2 * y + x for z in range(self.nz) for y in range(2)] for x in range(2)]

    def place(self, axis):
        return {"x": self.x, "y": self.y, "t": self.t}[axis]

    def swap(self, value, axis):
        if axis == "t":
            return lax.ppermute(value, "tensor", [(0, 1), (1, 0)])
        bit = {"x": 1, "y": 2}[axis]
        return lax.ppermute(value, "dp", [(i, i ^ bit) for i in range(self.n)])

    def shift(self, value, by):
        return lax.ppermute(value, "dp", [(i, (i + 4 * by) % self.n) for i in range(self.n)])

    def pair(self, mine, other, axis):
        here = self.place(axis)
        return jnp.where(here == 0, jnp.stack([mine, other]), jnp.stack([other, mine]))

    def pick(self, value, axis, dim, other=False):
        here = self.place(axis)
        return lax.dynamic_index_in_dim(value, 1 - here if other else here, dim, keepdims=False)

    def shifts(self, pieces):
        return [pieces[0]] + [self.shift(p, k) for k, p in enumerate(pieces) if k]

    def trade(self, value, axis):
        return self.pair(
            self.pick(value, axis, 0), self.swap(self.pick(value, axis, 0, True), axis), axis
        )

    def reduce(self, value, axis, dim):
        got = self.swap(self.pick(value, axis, dim, True).astype(BF16), axis)
        return self.pick(value, axis, dim).astype(F32) + got.astype(F32)

    def reduce_z(self, value):
        take = lambda k: lax.dynamic_index_in_dim(value, (self.z + k) % self.nz, 0, keepdims=False)
        total = take(0).astype(F32)
        for k in range(1, self.nz):
            total = total + self.shift(take(k).astype(BF16), k).astype(F32)
        return total


def local(n):
    def run(
        inputs,
        gain_mix,
        gain_mlp,
        branch_x,
        branch_y,
        conv_taps,
        conv_bias,
        gate_a,
        bias_a,
        gate_in,
        bias_in,
        decay_param,
        out_proj,
        ffn_gate,
        ffn_up,
        ffn_down,
        cotangent,
    ):
        grid = Grid(n)
        nz = grid.nz
        rows_each, width = inputs.shape
        part, half = branch_x.shape
        quarter = half // 2
        heads, gate_rows, block = gate_a.shape
        units = ffn_gate.shape[1] // nz
        split = part // 2
        run_len = nz * part
        length = 2 * rows_each
        slim = conv_bias.shape[0]
        here_x = grid.x == 0

        down_rows = jnp.transpose(ffn_down)
        slices = grid.shifts(cut((ffn_gate, ffn_up), grid.z, nz))

        vectors = jnp.concatenate(
            [conv_taps.reshape(-1), conv_bias, bias_a, bias_in, decay_param, gain_mix, gain_mlp]
        )
        pad_rows = -(2 * gate_rows + 1) % 16 + 1
        packed = jnp.concatenate(
            [
                jnp.transpose(gate_a, (1, 0, 2)).reshape(gate_rows, half),
                jnp.transpose(gate_in, (1, 0, 2)).reshape(gate_rows, half),
                jnp.pad(vectors[None], ((0, pad_rows - 1), (0, half - vectors.shape[0]))),
            ]
        )
        early = grid.shifts([after(packed[None], slices[1])] * nz)
        small = line_up(early, grid.z)[0]
        small = grid.pair(small, grid.swap(small, "y"), "y")
        small = grid.pair(small, grid.swap(small, "x"), "x")
        small = jnp.transpose(small, (2, 1, 0, 3, 4)).reshape(n, -1, half)
        gates = small[:, : 2 * gate_rows].reshape(n, 2, gate_rows, heads, block)
        gates = jnp.transpose(gates, (1, 3, 0, 2, 4)).reshape(2, heads, n * gate_rows, block)
        full_gate_a, full_gate_in = gates[0], gates[1]
        vecs = small[:, 2 * gate_rows].astype(F32)
        per = jnp.transpose(vecs[:, : 8 * slim].reshape(n, 8, slim), (1, 0, 2)).reshape(8, half)
        decay_row = per[7:8]
        per = jnp.concatenate([per[:7], jax.nn.softplus(decay_row)])
        full_gain_mix = vecs[:, 8 * slim : 8 * slim + part].reshape(width)
        full_gain_mlp = vecs[:, 8 * slim + part : 8 * slim + 2 * part].reshape(width)

        by_x = lambda w: jnp.stack([w[:, :quarter], w[:, quarter:]])
        mine = [by_x(w) for w in (branch_x, branch_y, jnp.transpose(out_proj))]
        mine = grid.trade(jnp.concatenate(mine, axis=-1), "x").reshape(2 * part, -1)
        mixer = lax.all_gather(mine, "dp", axis=0, tiled=True, axis_index_groups=grid.planes)
        full_in, full_out = mixer[:, : 2 * quarter], mixer[:, 2 * quarter :]
        across = grid.swap(after(inputs, mine), "x")

        normed = norm_rows(
            (inputs, grid.swap(inputs, "t")), (across, grid.swap(across, "t")), full_gain_mix, grid.t
        )

        def plane(own):
            return lax.all_gather(own, "dp", axis=0, tiled=True, axis_index_groups=grid.corners)

        slices = line_up(after(slices, normed, full_gate_a, full_gate_in, per), grid.z)[None]
        weights_pair = plane(after(slices, mixer))
        down_slices = grid.shifts(after(tuple(cut((down_rows,), grid.z, nz)), slices))

        def to_line(value, *deps):
            value = after(reorder(value, nz, False), *deps)
            return grid.shifts([value] * nz)

        rows = inputs.astype(F32)
        cot_line = to_line(cotangent, down_slices[1])
        pre = matmul(normed, full_in).reshape(2, length, 2 * quarter)

        def whole_half(mine, other):
            return jnp.where(
                here_x, jnp.concatenate([mine, other], 1), jnp.concatenate([other, mine], 1)
            )

        def to_rows(value):
            low, high = value[:, :quarter], value[:, quarter:]
            away = grid.swap(jnp.where(here_x, high, low), "x")
            return jnp.concatenate([jnp.where(here_x, low, high), away])

        got = grid.swap(pre[1].astype(BF16), "x").astype(F32)
        got = after(got, *down_slices[1:])
        weights_down = plane(after(line_up(down_slices, grid.z)[None], weights_pair))
        weights = (weights_pair, weights_down)
        pre_x = whole_half(pre[0, :, :quarter], got[:, :quarter])
        pre_y = whole_half(pre[0, :, quarter:], got[:, quarter:])
        mixed, states, conv, rate, entry = by_head(
            mixer_forward, heads, length, block, "rrggv", [("r", BF16)] + [("r", F32)] * 4, 30000000000
        )(pre_x, pre_y, full_gate_a, full_gate_in, per)
        mixed = after(to_rows(mixed), cot_line[1])
        branch_out = contract_last(mixed, full_out).reshape(2, 2, rows_each, width)
        branch_out = grid.reduce(branch_out, "t", 1)
        branch_out = branch_out[0] + grid.swap(branch_out[1].astype(BF16), "x").astype(F32)
        resid = after(rows + branch_out, *cot_line)

        normed_two_rows, norm_two_pull = jax.vjp(scale_norm, resid, full_gain_mlp)
        def from_line(acts, which, *deps):
            other = ffn_collect(acts[1], weights, which, BF16)
            other = grid.swap(other, "t")
            value = ffn_collect(acts[0], weights, which, F32) + other.astype(F32)
            value = after(value.reshape(nz, rows_each, width), *deps)
            away = [value[k].astype(BF16) for k in range(1, nz)]
            return away, [value[0]] + [grid.shift(v, -1 - k) for k, v in enumerate(away)]

        def total(got):
            return reorder(sum(g.astype(F32) for g in got), nz, True)

        def both_t(line):
            rows = jnp.concatenate(line)
            return rows, grid.swap(rows, "t")

        upstream = both_t(cot_line)
        normed_two = both_t(to_line(normed_two_rows.astype(BF16)))
        hidden, grad_pre = zip(
            *[ffn_middle(a, weights, u) for a, u in zip(normed_two, upstream)]
        )
        hidden = [h[None] for h in hidden]
        sent, got_result = from_line(hidden, (DOWN,))
        upstream, normed_two = after((upstream, normed_two), *sent)
        grad_ffn = weight_grad(normed_two, grad_pre, (), (nz, part), BF16, 3)
        grad_ffn = weight_grad(upstream, hidden, (), (nz, part), BF16, 3, 2, grad_ffn)
        grad_pre = after(grad_pre, grad_ffn, got_result[1])
        sent, got_two = from_line(grad_pre, (GATE, UP))

        def ffn_send(value, *deps):
            value = after(value, *deps)
            take = lambda k: lax.dynamic_index_in_dim(value, (grid.z + k) % nz, 1, keepdims=False)
            return grid.shifts([take(k) for k in range(nz)])

        grad_ffn = lax.psum_scatter(
            after(grad_ffn, got_result[1]), "dp", scatter_dimension=0, tiled=True, axis_index_groups=grid.corners
        )
        grad_normed_two = total(after(got_two, *got_result[1:]))
        grad_ffn = ffn_send(grad_ffn[0], got_two[1])

        grad_resid_norm, _ = norm_two_pull(grad_normed_two)
        grad_resid = cotangent.astype(F32) + grad_resid_norm
        back = grad_resid.astype(BF16)
        back = jnp.stack([back, grid.swap(back, "x")])
        back = jnp.swapaxes(grid.pair(back, grid.swap(back, "t"), "t"), 0, 1)
        back = back.reshape(2 * length, width)
        grad_mixed = matmul(back, full_out).reshape(2, length, quarter)
        grad_mixed = whole_half(
            grad_mixed[0], grid.swap(grad_mixed[1].astype(BF16), "x").astype(F32)
        )
        grad_mixed = after(grad_mixed, grad_ffn[1])
        grad_pre_y = gelu_parts(pre_y)[1] * (grad_mixed * states)
        grad_y_rows = to_rows(grad_pre_y.astype(BF16))

        def mixer_reduce(grad):
            grad = grad.reshape(nz, 2, 2, part, -1)
            away = grid.swap(grid.pick(grad, "y", 1, True).astype(BF16), "y")
            return grid.pick(grad, "y", 1), away

        def mixer_send(value, *deps):
            here, away = after(value, *deps)
            value = here + away.astype(F32)
            take = lambda k: lax.dynamic_index_in_dim(value, (grid.z + k) % nz, 0, keepdims=False)
            got = [take(0)] + [grid.shift(take(k).astype(BF16), k) for k in range(1, nz)]
            return got

        def mixer_finish(got):
            return grid.trade(got, "x")

        grad_oy = weight_grad([back], [mixed[None]], (2,), (2, part), BF16, 2)
        grad_oy = weight_grad([normed], [grad_y_rows[None]], (2,), (2, part), BF16, 2, 1, grad_oy)
        grad_oy = lax.psum_scatter(
            grad_oy.reshape(2 * nz, 2, 2, part, quarter),
            "dp",
            scatter_dimension=0,
            tiled=True,
            axis_index_groups=grid.planes,
        )[0]
        grad_pre_x, grad_gate_a, grad_gate_in, grad_vec = by_head(
            mixer_backward,
            heads,
            length,
            block,
            "rrrggvrrrr",
            [("r", BF16), ("w", F32), ("w", F32), ("v", F32)],
            30000000000,
        )(grad_mixed, pre_x, pre_y, full_gate_a, full_gate_in, per, states, conv, rate, entry)
        grad_vec = jnp.concatenate([grad_vec[:7], grad_vec[7:] * jax.nn.sigmoid(decay_row)])
        grad_x_rows = to_rows(grad_pre_x)
        grad_x = mixer_reduce(weight_grad([normed], [grad_x_rows[None]], (), (4, part), F32))
        grad_x = mixer_send(grad_x, *grad_ffn[1:])
        grad_in_rows = jnp.concatenate([grad_x_rows, grad_y_rows], axis=1)

        result = (resid + total(got_result)).astype(BF16)
        (grad_gate, grad_up, grad_down), sums = join(
            after(grad_ffn, *grad_x[1:]), (ffn_gate, ffn_up, down_rows), grid.z
        )
        grad_down = jnp.transpose(grad_down)
        grad_oy = after(grad_oy, *grad_x[1:])
        grad_out = mixer_finish(grad_oy[0])
        grad_out = jnp.transpose(grad_out, (0, 2, 1)).reshape(half, part).astype(F32)
        beside = lambda g: jnp.concatenate([g[0], g[1]], axis=1).astype(F32)
        grad_branch_y = beside(mixer_finish(grad_oy[1]))
        grad_x = sum(g.astype(F32) for g in grad_x).astype(BF16)
        grad_branch_x = beside(mixer_finish(grad_x))

        vec = jnp.transpose(grad_vec.reshape(8, n, slim), (1, 0, 2)).reshape(n, 1, 8 * slim)
        grad_small = jnp.concatenate(
            [
                grad_gate_a.reshape(n, gate_rows, half),
                grad_gate_in.reshape(n, gate_rows, half),
                jnp.pad(vec, ((0, 0), (0, pad_rows - 1), (0, half - 8 * slim))),
            ],
            axis=1,
        ).reshape(nz, 2, 2, 2 * gate_rows + pad_rows, half)
        grad_small = after(grad_small, grad_x_rows)
        grad_small = grid.reduce_z(grid.reduce(grid.reduce(grad_small, "x", 2), "y", 1))
        unpack = lambda g: jnp.transpose(g.reshape(gate_rows, heads, block), (1, 0, 2))
        vec = grad_small[2 * gate_rows, : 8 * slim].reshape(8, slim)

        grad_normed = contract_last(grad_in_rows, full_in).reshape(2, 2, rows_each, width)
        grad_normed = grid.reduce(grad_normed, "t", 1)
        grad_normed = grad_normed[0] + grid.swap(grad_normed[1].astype(BF16), "x").astype(F32)
        _, norm_pull = jax.vjp(scale_norm, rows, full_gain_mix)
        grad_rows, _ = norm_pull(grad_normed)
        grad_inputs = grad_resid + grad_rows

        gains = jnp.stack(
            [
                jnp.sum(
                    branch_x.astype(F32) * grad_branch_x + branch_y.astype(F32) * grad_branch_y,
                    axis=1,
                )
                / gain_mix.astype(F32),
                (sums[0] + sums[1])[:, 0]
                / gain_mlp.astype(F32),
            ]
        )
        gains = gains + grid.swap(gains, "t")
        gains = lax.dynamic_index_in_dim(gains.reshape(2, 2, split), grid.t, 1, keepdims=False)
        return (
            result,
            grad_inputs,
            gains[0],
            gains[1],
            grad_branch_x,
            grad_branch_y,
            vec[:4],
            vec[4],
            unpack(grad_small[:gate_rows]),
            vec[5],
            unpack(grad_small[gate_rows : 2 * gate_rows]),
            vec[6],
            vec[7],
            grad_out,
            grad_gate,
            grad_up,
            grad_down,
        )

    return run


def solution(mesh):
    in_specs = (
        P(("dp", "tensor"), None),
        P("dp"),
        P("dp"),
        P("dp", "tensor"),
        P("dp", "tensor"),
        P(None, ("tensor", "dp")),
        P(("tensor", "dp")),
        P("tensor", "dp", None),
        P(("tensor", "dp")),
        P("tensor", "dp", None),
        P(("tensor", "dp")),
        P(("tensor", "dp")),
        P("tensor", "dp"),
        P("dp", "tensor"),
        P("dp", "tensor"),
        P("tensor", "dp"),
        P(("dp", "tensor"), None),
    )
    out_specs = (
        P(("dp", "tensor"), None),
        P(("dp", "tensor"), None),
        P(("dp", "tensor")),
        P(("dp", "tensor")),
        P("dp", "tensor"),
        P("dp", "tensor"),
        P(None, ("tensor", "dp")),
        P(("tensor", "dp")),
        P("tensor", "dp", None),
        P(("tensor", "dp")),
        P("tensor", "dp", None),
        P(("tensor", "dp")),
        P(("tensor", "dp")),
        P("tensor", "dp"),
        P("dp", "tensor"),
        P("dp", "tensor"),
        P("tensor", "dp"),
    )
    return jax.shard_map(
        local(mesh.shape["dp"]),
        mesh=mesh,
        in_specs=in_specs,
        out_specs=out_specs,
        check_vma=False,
    )
```
